32 devices in a mesh: seq: 8 (over y, x, core), head: 4 (over z).
Axes of the slice: x: 2, y: 2, z: 4, core: 2. Of those that a mesh axis runs over, the one named last changes fastest.
Arguments:
- queries: bfloat16 [2048, 4096], P(('seq', 'head')), may hold values from -72 to 72
- keys: bfloat16 [2048, 2048], P(('seq', 'head')), may hold values from -6 to 6
- values: bfloat16 [2048, 2048], P(('seq', 'head')), may hold values from -6 to 6
- prefix_keys: bfloat16 [4096, 2048], P(None, 'head'), may hold values from -10 to 10
- prefix_values: bfloat16 [4096, 2048], P(None, 'head'), may hold values from -6 to 6
- span_start: int32 [1], replicated, may hold values from 0 to 4095
Outputs:
- attended: bfloat16 [2048, 4096], P(('seq', 'head'))
The draws below stay inside these ranges and needn't reach their ends.
All inputs are finite; a program needn't handle non-finite values.
Results may differ from the reference program's by a relative error of at most 0.003.
Values may be sent and summed in bfloat16 or wider, within the bound.
No kernel may reach another device: no remote copies, remote signals or barrier semaphores. Data moves between devices by JAX's collectives and lax.ppermute only.
A program may use at most 128 MiB of HBM per device.

```python
import jax
import jax.numpy as jnp
from jax import lax

HEAD_DIM = 128
QH = 32
KVH = 16
QSCALE = 144
WINDOW = 4096
TOKENS = 2048
BLOCK = 256


def base_keys(key):
    raw = jax.random.normal(jax.random.fold_in(key, 7), (TOKENS, KVH * HEAD_DIM), jnp.float32)
    return jnp.clip(1.7 * raw, -6.0, 6.0)


def draw_keys(key, part):
    result = base_keys(key)
    return result.astype(jnp.bfloat16)


def draw_queries(key, part):
    raw = jax.random.normal(jax.random.fold_in(key, 11), (TOKENS, QH * HEAD_DIM), jnp.float32)
    result = jnp.clip(1.7 * raw, -6.0, 6.0)
    return result.astype(jnp.bfloat16)


def levels(rng, extent, pieces, least, top_value):
    loudness, own = 1.0, jax.random.fold_in(rng, 6)
    for dim, shards_of in pieces:
        steps = jnp.exp(jax.random.uniform(jax.random.fold_in(own, dim), (shards_of,), jnp.float32, least / len(pieces), top_value / len(pieces)))
        loudness = loudness * jnp.repeat(steps, extent[dim] // shards_of).reshape([-1 if axis == dim else 1 for axis in range(len(extent))])
    return loudness


def gaussian(key, shape, deviation, limit, split=(), kind=jnp.bfloat16):
    drawn = jax.random.normal(key, shape, jnp.float32) * deviation
    if len(split) > 0:
        drawn = levels(key, shape, split, -0.22, 0.18) * drawn
    return jnp.clip(drawn, min=-limit, max=limit).astype(kind)


def setup_inputs(seed: int = 0) -> dict:
    arg_keys = jax.random.split(jax.random.key(seed), 7)
    queries = draw_queries(jax.random.fold_in(arg_keys[6], 71), 0)
    keys = draw_keys(jax.random.fold_in(arg_keys[6], 71), 0)
    values = gaussian(arg_keys[2], (TOKENS, KVH * HEAD_DIM), 1.0, 6.0, ((0, 32),))
    prefix_keys = gaussian(arg_keys[3], (WINDOW, KVH * HEAD_DIM), 1.7, 10.0, ((1, 4),))
    prefix_values = gaussian(arg_keys[4], (WINDOW, KVH * HEAD_DIM), 1.0, 6.0, ((1, 4),))
    span_start = jax.random.randint(arg_keys[5], (1,), 0, WINDOW).astype(jnp.int32)
    return {"queries": queries, "keys": keys, "values": values, "prefix_keys": prefix_keys, "prefix_values": prefix_values, "span_start": span_start}


def attend_exact(query_rows, key_rows, value_rows, query_first, key_first, start_value):
    block_rows = query_rows.shape[0]
    key_count = key_rows.shape[0]
    grouping = QH // KVH
    scaling = QSCALE ** -0.5
    query_pos = query_first + jnp.arange(block_rows, dtype=jnp.int32)
    key_pos = key_first + jnp.arange(key_count, dtype=jnp.int32)
    distance = query_pos[:, None] - key_pos[None, :]
    allowed = (distance >= 0) & (distance < WINDOW) & ((start_value + key_pos) >= 0)[None, :]
    outputs = []
    for key_group in range(KVH):
        lower = key_group * grouping * HEAD_DIM
        query_head = query_rows[:, lower:lower + grouping * HEAD_DIM].reshape(block_rows, grouping, HEAD_DIM).astype(jnp.float32)
        key_head = key_rows[:, key_group * HEAD_DIM:(key_group + 1) * HEAD_DIM].astype(jnp.float32)
        value_head = value_rows[:, key_group * HEAD_DIM:(key_group + 1) * HEAD_DIM].astype(jnp.float32)
        scores = jnp.einsum("qgd,kd->gqk", query_head, key_head) * scaling
        scores = jnp.where(allowed[None], scores, -jnp.inf)
        peak_score = jnp.max(scores, axis=2, keepdims=True)
        unnormed = jnp.where(allowed[None], jnp.exp(scores - peak_score), jnp.float32(0.0))
        totals = jnp.sum(unnormed, axis=2)
        weights = lax.optimization_barrier(unnormed.astype(jnp.bfloat16)).astype(jnp.float32)
        mixture = jnp.einsum("gqk,kd->qgd", weights, value_head)
        outputs.append((mixture / jnp.transpose(totals)[:, :, None]).reshape(block_rows, grouping * HEAD_DIM))
    return jnp.concatenate(outputs, axis=1).astype(jnp.bfloat16)


def reference(queries, keys, values, prefix_keys, prefix_values, span_start):
    all_keys = jnp.concatenate([prefix_keys, keys], axis=0)
    all_values = jnp.concatenate([prefix_values, values], axis=0)
    start_value = span_start[0]

    def one_block(block_index):
        first = block_index * BLOCK
        query_rows = lax.dynamic_slice_in_dim(queries, first, BLOCK, 0)
        key_rows = lax.dynamic_slice_in_dim(all_keys, first, WINDOW + BLOCK, 0)
        value_rows = lax.dynamic_slice_in_dim(all_values, first, WINDOW + BLOCK, 0)
        return attend_exact(query_rows, key_rows, value_rows, first, first - WINDOW, start_value)

    blocks = lax.map(one_block, jnp.arange(TOKENS // BLOCK, dtype=jnp.int32))
    return blocks.reshape(TOKENS, QH * HEAD_DIM)
```

```python
import functools

import jax
import jax.numpy as jnp
from jax import lax
from jax.experimental import pallas as pl
from jax.experimental.pallas import tpu as pltpu
from jax.sharding import PartitionSpec as P

HEAD_DIM = 128
QH = 32
KVH = 16
QSCALE = 144
WINDOW = 4096
LOG2E = 1.4426950408889634
NEG = -1e30


def shifted(shard, axis, by):
    size = lax.axis_size(axis)
    pairs = [(i, i + by) for i in range(size) if 0 <= i + by < size]
    return lax.ppermute(shard, axis, pairs)


def shortened(shard):
    return jax.tree.map(lambda a: a.astype(jnp.bfloat16) if a.dtype == jnp.float32 else a, shard)


def attend_block(query_rows, key_rows, value_rows, query_first, key_first, start_value):
    block_rows = query_rows.shape[0]
    key_count = key_rows.shape[0]
    grouping = QH // KVH
    scaling = QSCALE ** (-0.5)
    local_groups = key_rows.shape[1] // HEAD_DIM
    query_pos = query_first + jnp.arange(block_rows, dtype=jnp.int32)
    key_pos = key_first + jnp.arange(key_count, dtype=jnp.int32)
    distance = query_pos[:, None] - key_pos[None, :]
    allowed = (distance >= 0) & (distance < WINDOW) & (start_value + key_pos >= 0)[None, :]
    outputs = []
    for key_group in range(local_groups):
        lower = key_group * grouping * HEAD_DIM
        query_head = query_rows[:, lower : lower + grouping * HEAD_DIM].reshape(
            block_rows, grouping, HEAD_DIM
        )
        key_head = key_rows[:, key_group * HEAD_DIM : (key_group + 1) * HEAD_DIM]
        value_head = value_rows[:, key_group * HEAD_DIM : (key_group + 1) * HEAD_DIM]
        scores = (
            jnp.einsum("qgd,kd->gqk", query_head, key_head, preferred_element_type=jnp.float32)
            * scaling
        )
        scores = jnp.where(allowed[None], scores, -jnp.inf)
        peak_score = jnp.max(scores, axis=2, keepdims=True)
        unnormed = jnp.exp(scores - peak_score)
        totals = jnp.sum(unnormed, axis=2)
        weights = unnormed.astype(jnp.bfloat16)
        mixture = jnp.einsum("gqk,kd->qgd", weights, value_head, preferred_element_type=jnp.float32)
        outputs.append(
            (mixture / jnp.transpose(totals)[:, :, None]).reshape(block_rows, grouping * HEAD_DIM)
        )
    return jnp.concatenate(outputs, axis=1).astype(jnp.bfloat16)


def relayed_shards(queries, keys, values, prefix_keys, prefix_values, span_start):
    query_local, key_local, value_local = (
        lax.all_to_all(queries, "head", split_axis=1, concat_axis=0, tiled=True),
        lax.all_to_all(keys, "head", split_axis=1, concat_axis=0, tiled=True),
        lax.all_to_all(values, "head", split_axis=1, concat_axis=0, tiled=True),
    )
    seq_rows = query_local.shape[0]
    shards_back = WINDOW // seq_rows
    seq_index = lax.axis_index("seq")

    def relay(step, carried):
        moving_keys, moving_values, window_keys, window_values = carried
        moving_keys, moving_values = shifted((moving_keys, moving_values), "seq", 1)
        offset = (shards_back - 1 - step) * seq_rows
        window_keys = lax.dynamic_update_slice_in_dim(window_keys, moving_keys, offset, 0)
        window_values = lax.dynamic_update_slice_in_dim(window_values, moving_values, offset, 0)
        return (moving_keys, moving_values, window_keys, window_values)

    empty = jnp.zeros((WINDOW, key_local.shape[1]), jnp.bfloat16)
    carried = lax.fori_loop(0, shards_back, relay, (key_local, value_local, empty, empty))
    window_keys = carried[2]
    window_values = carried[3]
    first_row = jnp.minimum(seq_index * seq_rows, WINDOW)
    padded_keys = jnp.concatenate([prefix_keys, jnp.zeros_like(prefix_keys)], axis=0)
    padded_values = jnp.concatenate([prefix_values, jnp.zeros_like(prefix_values)], axis=0)
    window_keys = window_keys + lax.dynamic_slice_in_dim(padded_keys, first_row, WINDOW, 0)
    window_values = window_values + lax.dynamic_slice_in_dim(padded_values, first_row, WINDOW, 0)
    all_keys = jnp.concatenate([window_keys, key_local], axis=0)
    all_values = jnp.concatenate([window_values, value_local], axis=0)
    block_rows = min(512, seq_rows)
    block_count = seq_rows // block_rows
    start_value = span_start[0]
    key_base = (seq_index - shards_back) * seq_rows
    query_base = seq_index * seq_rows

    def one_block(block_index):
        first = block_index * block_rows
        return attend_block(
            query_local, all_keys, all_values, query_base + first, key_base + first, start_value
        )

    blocks = lax.map(one_block, jnp.arange(block_count, dtype=jnp.int32))
    attended = blocks.reshape(seq_rows, query_local.shape[1])
    return lax.all_to_all(
        shortened(attended), "head", split_axis=0, concat_axis=1, tiled=True
    ).astype(attended.dtype)


def attend(start_ref, col_ref, q_ref, k_ref, v_ref, pk_hbm, pv_hbm, o_ref, k_all, v_all, s_buf, m_buf, acc, sems, *, W, T, R, scale):
    col = pl.multiple_of(col_ref[0]*HEAD_DIM, HEAD_DIM)
    nchunk = W // R
    t0 = W - start_ref[0]
    ck = pltpu.make_async_copy(pk_hbm.at[:, pl.ds(col, HEAD_DIM)], k_all.at[pl.ds(0, W)], sems.at[0])
    cv = pltpu.make_async_copy(pv_hbm.at[:, pl.ds(col, HEAD_DIM)], v_all.at[pl.ds(0, W), pl.ds(0, HEAD_DIM)], sems.at[1])
    ck.start(); cv.start()
    k_all[W:, :] = k_ref[...]
    v_all[W:, :HEAD_DIM] = v_ref[...]
    v_all[:, HEAD_DIM:] = jnp.ones((W+T, HEAD_DIM), jnp.bfloat16)
    ck.wait(); cv.wait()
    rows = lax.broadcasted_iota(jnp.int32, (R, R), 0)
    lanes = lax.broadcasted_iota(jnp.int32, (R, R), 1)

    def qk(q, kc):
        k = k_all[pl.ds(pl.multiple_of(kc*R, R), R), :]
        return lax.dot_general(q, k, (((1,),(1,)),((),())), preferred_element_type=jnp.float32)
    def lanemax(s):
        m = s[:, :128]
        for j in range(1, R//128): m = jnp.maximum(m, s[:, j*128:(j+1)*128])
        return m

    def block(b, _):
        q = q_ref[pl.ds(pl.multiple_of(b*R, R), R), :]
        first = jnp.maximum(b, t0 // R)
        last = b + nchunk
        s = qk(q, last)
        lo = jnp.maximum(rows + b*R + 1, t0) - last*R
        s = jnp.where((lanes <= rows) & (lanes >= lo), s, -jnp.inf)
        s_buf[nchunk] = s
        m_buf[...] = jnp.maximum(lanemax(s), NEG)
        @pl.when(first < last)
        def _():
            s = qk(q, first)
            lo = jnp.maximum(rows + b*R + 1, t0) - first*R
            s = jnp.where(lanes >= lo, s, -jnp.inf)
            s_buf[first-b] = s
            m_buf[...] = jnp.maximum(m_buf[...], lanemax(s))
        def one(kc, _):
            s = qk(q, kc)
            s_buf[kc-b] = s
            m_buf[...] = jnp.maximum(m_buf[...], lanemax(s))
            return 0
        lax.fori_loop(first+1, last, one, 0)
        mc = jnp.max(m_buf[...], axis=1, keepdims=True) * scale
        acc[...] = jnp.zeros_like(acc)
        def two(kc, _):
            p = jnp.exp2(s_buf[kc-b]*scale - mc).astype(jnp.bfloat16)
            acc[...] += jnp.dot(p, v_all[pl.ds(pl.multiple_of(kc*R, R), R), :], preferred_element_type=jnp.float32)
            return 0
        lax.fori_loop(first, last+1, two, 0)
        o_ref[pl.ds(pl.multiple_of(b*R, R), R), :] = (acc[:, :HEAD_DIM] / acc[:, HEAD_DIM:]).astype(o_ref.dtype)
        return 0
    lax.fori_loop(0, T//R, block, 0)

def call(start, col, q, k, v, pk, pv, R=512):
    T=q.shape[0]; W=pk.shape[0]
    vm = pl.BlockSpec(memory_space=pltpu.VMEM); sm = pl.BlockSpec(memory_space=pltpu.SMEM); an = pl.BlockSpec(memory_space=pl.ANY)
    return pl.pallas_call(functools.partial(attend, W=W, T=T, R=R, scale=LOG2E*QSCALE**-0.5),
        out_shape=jax.ShapeDtypeStruct((T, HEAD_DIM), jnp.bfloat16),
        in_specs=[sm, sm, vm, vm, vm, an, an], out_specs=vm,
        scratch_shapes=[pltpu.VMEM((W+T, HEAD_DIM), jnp.bfloat16), pltpu.VMEM((W+T, 2*HEAD_DIM), jnp.bfloat16),
            pltpu.VMEM((W//R+1, R, R), jnp.float32), pltpu.VMEM((R,128), jnp.float32), pltpu.VMEM((R, 2*HEAD_DIM), jnp.float32), pltpu.SemaphoreType.DMA((2,))],
        compiler_params=pltpu.CompilerParams(vmem_limit_bytes=48*2**20),
        cost_estimate=pl.CostEstimate(flops=10**10, bytes_accessed=2**22, transcendentals=10**7),
        name="attend")(start, col, q, k, v, pk, pv)
BOTH = ("seq", "head")


def spread_shards(queries, keys, values, prefix_keys, prefix_values, span_start):
    rows = queries.shape[0]
    seq_size, head_size = lax.axis_size("seq"), lax.axis_size("head")
    seq_index = lax.axis_index("seq")
    pairs = seq_size // 2
    q = queries.reshape(rows, head_size, seq_size, HEAD_DIM).transpose(2, 1, 0, 3)
    q = q.reshape(seq_size * head_size, rows, HEAD_DIM)
    kv = jnp.stack([keys, values]).reshape(2, rows, head_size, pairs, HEAD_DIM)
    kv = kv.transpose(3, 0, 2, 1, 4).reshape(seq_size * head_size, rows, HEAD_DIM)
    packed = jnp.concatenate([q, kv], axis=2)
    got = lax.all_to_all(packed, BOTH, split_axis=0, concat_axis=0, tiled=True)
    tokens = seq_size * head_size * rows
    got = got.reshape(tokens, 2 * HEAD_DIM)
    query_head, mine = got[:, :HEAD_DIM], got[:, HEAD_DIM:]
    other = lax.ppermute(mine, "seq", [(i, i ^ 1) for i in range(seq_size)])
    has_keys = seq_index % 2 == 0
    key_head = jnp.where(has_keys, mine, other)
    value_head = jnp.where(has_keys, other, mine)
    column = (seq_index // 2).astype(jnp.int32).reshape(1)
    attended = call(span_start, column, query_head, key_head, value_head, prefix_keys, prefix_values)
    attended = attended.reshape(seq_size * head_size, rows, HEAD_DIM)
    back = lax.all_to_all(attended, BOTH, split_axis=0, concat_axis=0, tiled=True)
    back = back.reshape(seq_size, head_size, rows, HEAD_DIM).transpose(2, 1, 0, 3)
    return back.reshape(rows, QH * HEAD_DIM)


def solution(mesh):
    placed = (
        P(("seq", "head"), None),
        P(("seq", "head"), None),
        P(("seq", "head"), None),
        P(None, "head"),
        P(None, "head"),
        P(),
    )
    spread = mesh.shape["seq"] * mesh.shape["head"] == QH and QH == 2 * KVH
    shards = spread_shards if spread else relayed_shards
    return jax.shard_map(
        shards, mesh=mesh, in_specs=placed, out_specs=P(("seq", "head"), None), check_vma=False
    )
```

```python
import functools

import jax
import jax.numpy as jnp
from jax import lax
from jax.experimental import pallas as pl
from jax.experimental.pallas import tpu as pltpu
from jax.sharding import PartitionSpec as P

HEAD_DIM = 128
QH = 32
KVH = 16
QSCALE = 144
WINDOW = 4096
GROUPING = QH // KVH
EXP2_SCALE = 1.4426950408889634 * QSCALE**-0.5
LOWEST = -1e30
ONES_ROWS = 16
V_ROWS = HEAD_DIM + ONES_ROWS
PREFIX_TILE = 1024
SPAN_TILE = 1024


def shifted(shard, axis, by):
    size = lax.axis_size(axis)
    pairs = [(i, i + by) for i in range(size) if 0 <= i + by < size]
    return lax.ppermute(shard, axis, pairs)


def shortened(shard):
    return jax.tree.map(lambda a: a.astype(jnp.bfloat16) if a.dtype == jnp.float32 else a, shard)


def attend_block(query_rows, key_rows, value_rows, query_first, key_first, start_value):
    block_rows = query_rows.shape[0]
    key_count = key_rows.shape[0]
    grouping = QH // KVH
    scaling = QSCALE ** (-0.5)
    local_groups = key_rows.shape[1] // HEAD_DIM
    query_pos = query_first + jnp.arange(block_rows, dtype=jnp.int32)
    key_pos = key_first + jnp.arange(key_count, dtype=jnp.int32)
    distance = query_pos[:, None] - key_pos[None, :]
    allowed = (distance >= 0) & (distance < WINDOW) & (start_value + key_pos >= 0)[None, :]
    outputs = []
    for key_group in range(local_groups):
        lower = key_group * grouping * HEAD_DIM
        query_head = query_rows[:, lower : lower + grouping * HEAD_DIM].reshape(
            block_rows, grouping, HEAD_DIM
        )
        key_head = key_rows[:, key_group * HEAD_DIM : (key_group + 1) * HEAD_DIM]
        value_head = value_rows[:, key_group * HEAD_DIM : (key_group + 1) * HEAD_DIM]
        scores = (
            jnp.einsum("qgd,kd->gqk", query_head, key_head, preferred_element_type=jnp.float32)
            * scaling
        )
        scores = jnp.where(allowed[None], scores, -jnp.inf)
        peak_score = jnp.max(scores, axis=2, keepdims=True)
        unnormed = jnp.exp(scores - peak_score)
        totals = jnp.sum(unnormed, axis=2)
        weights = unnormed.astype(jnp.bfloat16)
        mixture = jnp.einsum("gqk,kd->qgd", weights, value_head, preferred_element_type=jnp.float32)
        outputs.append(
            (mixture / jnp.transpose(totals)[:, :, None]).reshape(block_rows, grouping * HEAD_DIM)
        )
    return jnp.concatenate(outputs, axis=1).astype(jnp.bfloat16)


def relayed_shards(queries, keys, values, prefix_keys, prefix_values, span_start):
    query_local, key_local, value_local = (
        lax.all_to_all(queries, "head", split_axis=1, concat_axis=0, tiled=True),
        lax.all_to_all(keys, "head", split_axis=1, concat_axis=0, tiled=True),
        lax.all_to_all(values, "head", split_axis=1, concat_axis=0, tiled=True),
    )
    seq_rows = query_local.shape[0]
    shards_back = WINDOW // seq_rows
    seq_index = lax.axis_index("seq")

    def relay(step, carried):
        moving_keys, moving_values, window_keys, window_values = carried
        moving_keys, moving_values = shifted((moving_keys, moving_values), "seq", 1)
        offset = (shards_back - 1 - step) * seq_rows
        window_keys = lax.dynamic_update_slice_in_dim(window_keys, moving_keys, offset, 0)
        window_values = lax.dynamic_update_slice_in_dim(window_values, moving_values, offset, 0)
        return (moving_keys, moving_values, window_keys, window_values)

    empty = jnp.zeros((WINDOW, key_local.shape[1]), jnp.bfloat16)
    carried = lax.fori_loop(0, shards_back, relay, (key_local, value_local, empty, empty))
    window_keys = carried[2]
    window_values = carried[3]
    first_row = jnp.minimum(seq_index * seq_rows, WINDOW)
    padded_keys = jnp.concatenate([prefix_keys, jnp.zeros_like(prefix_keys)], axis=0)
    padded_values = jnp.concatenate([prefix_values, jnp.zeros_like(prefix_values)], axis=0)
    window_keys = window_keys + lax.dynamic_slice_in_dim(padded_keys, first_row, WINDOW, 0)
    window_values = window_values + lax.dynamic_slice_in_dim(padded_values, first_row, WINDOW, 0)
    all_keys = jnp.concatenate([window_keys, key_local], axis=0)
    all_values = jnp.concatenate([window_values, value_local], axis=0)
    block_rows = min(512, seq_rows)
    block_count = seq_rows // block_rows
    start_value = span_start[0]
    key_base = (seq_index - shards_back) * seq_rows
    query_base = seq_index * seq_rows

    def one_block(block_index):
        first = block_index * block_rows
        return attend_block(
            query_local, all_keys, all_values, query_base + first, key_base + first, start_value
        )

    blocks = lax.map(one_block, jnp.arange(block_count, dtype=jnp.int32))
    attended = blocks.reshape(seq_rows, query_local.shape[1])
    return lax.all_to_all(
        shortened(attended), "head", split_axis=0, concat_axis=1, tiled=True
    ).astype(attended.dtype)


def in_vmem():
    return pl.BlockSpec(memory_space=pltpu.VMEM)


def in_smem():
    return pl.BlockSpec(memory_space=pltpu.SMEM)


def anywhere():
    return pl.BlockSpec(memory_space=pl.ANY)


def params():
    return pltpu.CompilerParams(vmem_limit_bytes=40 * 2**20)


def lanes(index, width):
    return pl.ds(pl.multiple_of(index * width, width), width)


def split_planes(queries, keys, values):
    rows = queries.shape[0]
    planes = lax.axis_size("head")
    q_width, kv_width = queries.shape[1] // planes, keys.shape[1] // planes

    def kernel(q_ref, k_ref, v_ref, *rest):
        kv_out, q_out, sems = rest[:planes], rest[planes : 2 * planes], rest[2 * planes]
        here = lax.axis_index("head")
        copies = []
        for r in range(planes):
            plane = here ^ r
            for source, width, target in (
                (k_ref, kv_width, kv_out[r].at[:, pl.ds(0, kv_width)]),
                (v_ref, kv_width, kv_out[r].at[:, pl.ds(kv_width, kv_width)]),
                (q_ref, q_width, q_out[r]),
            ):
                copy = pltpu.make_async_copy(
                    source.at[:, lanes(plane, width)], target, sems.at[len(copies)]
                )
                copy.start()
                copies.append(copy)
        for copy in copies:
            copy.wait()

    out = [jax.ShapeDtypeStruct((rows, 2 * kv_width), jnp.bfloat16)] * planes
    out += [jax.ShapeDtypeStruct((rows, q_width), jnp.bfloat16)] * planes
    result = pl.pallas_call(
        kernel,
        out_shape=out,
        in_specs=[anywhere()] * 3,
        out_specs=[in_vmem()] * (2 * planes),
        scratch_shapes=[pltpu.SemaphoreType.DMA((3 * planes,))],
        compiler_params=params(),
        name="split_planes",
    )(queries, keys, values)
    return result[:planes], result[planes:]


def join_planes(pieces):
    rows, width = pieces[0].shape
    planes = len(pieces)

    def kernel(*refs):
        out_ref, sems = refs[planes], refs[planes + 1]
        here = lax.axis_index("head")
        copies = []
        for r in range(planes):
            copy = pltpu.make_async_copy(
                refs[r], out_ref.at[:, lanes(here ^ r, width)], sems.at[r]
            )
            copy.start()
            copies.append(copy)
        for copy in copies:
            copy.wait()

    return pl.pallas_call(
        kernel,
        out_shape=jax.ShapeDtypeStruct((rows, planes * width), jnp.bfloat16),
        in_specs=[in_vmem()] * planes,
        out_specs=anywhere(),
        scratch_shapes=[pltpu.SemaphoreType.DMA((planes,))],
        compiler_params=params(),
        name="join_planes",
    )(*pieces)


def turn_prefix_values(prefix_values):
    count, width = prefix_values.shape
    heads = width // HEAD_DIM

    def kernel(v_ref, out_ref):
        out_ref[:, HEAD_DIM:, :] = jnp.ones((heads, ONES_ROWS, count), jnp.bfloat16)

        def turn(chunk, _):
            at = lanes(chunk, 512)
            for g in range(heads):
                out_ref[g, :HEAD_DIM, at] = v_ref[at, g * HEAD_DIM : (g + 1) * HEAD_DIM].T
            return 0

        lax.fori_loop(0, count // 512, turn, 0)

    return pl.pallas_call(
        kernel,
        out_shape=jax.ShapeDtypeStruct((heads, V_ROWS, count), jnp.bfloat16),
        in_specs=[in_vmem()],
        out_specs=in_vmem(),
        compiler_params=params(),
        cost_estimate=pl.CostEstimate(flops=0, bytes_accessed=2**23, transcendentals=0),
        name="turn_prefix_values",
    )(prefix_values)


def stack_pair(first, second):
    rows, width = first.shape
    heads = width // (2 * HEAD_DIM)

    def kernel(a_ref, b_ref, out_ref):
        for g in range(2 * heads):
            at = slice(g * HEAD_DIM, (g + 1) * HEAD_DIM)
            both = jnp.concatenate([a_ref[:, at], b_ref[:, at]], axis=0)
            out_ref[g] = both if g < heads else both.T

    return pl.pallas_call(
        kernel,
        out_shape=jax.ShapeDtypeStruct((2 * heads, 2 * rows, HEAD_DIM), jnp.bfloat16),
        in_specs=[in_vmem()] * 2,
        out_specs=in_vmem(),
        compiler_params=params(),
        cost_estimate=pl.CostEstimate(flops=0, bytes_accessed=2**21, transcendentals=0),
        name="stack_pair",
    )(first, second)


def tile_of_heads(heads, scores_of, values_of, allowed, m_ref, acc_ref, opening):
    scores = scores_of(0)
    for g in range(heads):
        now = scores
        if g + 1 < heads:
            scores = scores_of(g + 1)
        if allowed is not None:
            now = jnp.where(allowed, now, -jnp.inf)
        peak = jnp.max(now, axis=0, keepdims=True)
        before = None if opening else m_ref[g, :1, :]
        peak = jnp.maximum(peak, LOWEST if opening else before)
        scaled = peak * EXP2_SCALE
        weights = jnp.exp2(now * EXP2_SCALE - scaled).astype(jnp.bfloat16)
        sums = jnp.dot(values_of(g), weights, preferred_element_type=jnp.float32)
        if not opening:
            sums = sums + acc_ref[g] * jnp.exp2(before * EXP2_SCALE - scaled)
        acc_ref[g] = sums
        m_ref[g] = jnp.broadcast_to(peak, m_ref.shape[1:])


def dot_turned(keys, queries):
    return lax.dot_general(
        keys, queries, (((1,), (1,)), ((), ())), preferred_element_type=jnp.float32
    )


def attend_prefix(span_start, pieces, prefix_keys, turned_values):
    rows, width = pieces[0].shape
    planes = len(pieces)
    window = prefix_keys.shape[0]
    heads = prefix_keys.shape[1] // HEAD_DIM
    block = planes * rows
    columns = GROUPING * block
    size = PREFIX_TILE

    def kernel(start_ref, *refs):
        q_refs = refs[:planes]
        k_ref, v_ref, q_all, m_ref, acc_ref = refs[planes:]
        for r in range(planes):
            for h in range(heads * GROUPING):
                at = (h % GROUPING) * block + r * rows
                q_all[h // GROUPING, at : at + rows, :] = q_refs[r][
                    :, h * HEAD_DIM : (h + 1) * HEAD_DIM
                ]
        first_query = lax.axis_index("seq") * block
        turn = lax.axis_index("head") * rows
        first_key = window - start_ref[0]
        lowest = jnp.maximum(first_query + 1, first_key)
        tiles = (window - lowest + size - 1) // size

        def tile(j, masked):
            row = pl.multiple_of(window - (j + 1) * size, size)
            allowed = None
            if masked:
                key = lax.broadcasted_iota(jnp.int32, (size, columns), 0)
                place = lax.broadcasted_iota(jnp.int32, (1, columns), 1) % block
                query = first_query + (place ^ turn)
                allowed = key >= jnp.maximum(query + 1, first_key) - row
            tile_of_heads(
                heads,
                lambda g: dot_turned(
                    k_ref[pl.ds(row, size), g * HEAD_DIM : (g + 1) * HEAD_DIM], q_all[g]
                ),
                lambda g: v_ref[g, :, pl.ds(row, size)],
                allowed,
                m_ref,
                acc_ref,
                masked,
            )

        @pl.when(tiles == 0)
        def _():
            m_ref[...] = jnp.full(m_ref.shape, LOWEST, jnp.float32)
            acc_ref[...] = jnp.zeros(acc_ref.shape, jnp.float32)

        @pl.when(tiles > 0)
        def _():
            tile(tiles - 1, True)

        def one(j, _):
            tile(j, False)
            return 0

        lax.fori_loop(0, tiles - 1, one, 0)

    return pl.pallas_call(
        kernel,
        out_shape=[
            jax.ShapeDtypeStruct((heads, columns, HEAD_DIM), jnp.bfloat16),
            jax.ShapeDtypeStruct((heads, 8, columns), jnp.float32),
            jax.ShapeDtypeStruct((heads, V_ROWS, columns), jnp.float32),
        ],
        in_specs=[in_smem()] + [in_vmem()] * (planes + 2),
        out_specs=[in_vmem()] * 3,
        compiler_params=params(),
        cost_estimate=pl.CostEstimate(
            flops=4 * heads * columns * window * HEAD_DIM, bytes_accessed=2**23,
            transcendentals=heads * columns * window
        ),
        name="attend_prefix",
    )(span_start, *pieces, prefix_keys, turned_values)


def attend_span(q_all, m, acc, sources):
    heads, columns, _ = q_all.shape
    block = columns // GROUPING
    half_rows = sources[0][0].shape[1]
    halves = block // half_rows
    blocks = len(sources)
    tokens = blocks * block
    planes = lax.axis_size("head")
    rows = block // planes
    size = min(SPAN_TILE, tokens)
    flat = [piece for source in sources for piece in source]

    def kernel(q_ref, m_in, acc_in, *refs):
        kv_refs = refs[: len(flat)]
        o_refs = refs[len(flat) : len(flat) + planes]
        m_ref, acc_ref, k_all, v_all = refs[len(flat) + planes :]
        me = lax.axis_index("seq")
        turn = lax.axis_index("head") * rows
        m_ref[...] = m_in[...]
        acc_ref[...] = acc_in[...]
        v_all[:, HEAD_DIM:, :] = jnp.ones((heads, ONES_ROWS, tokens), jnp.bfloat16)
        for index, piece in enumerate(kv_refs):
            at = lanes((me ^ (index // halves)) * halves + index % halves, half_rows)
            for g in range(heads):
                k_all[g, at, :] = piece[g]
                v_all[g, :HEAD_DIM, at] = piece[heads + g]
        last = me * block // size

        def tile(j, masked):
            row = pl.multiple_of(j * size, size)
            allowed = None
            if masked:
                key = row + lax.broadcasted_iota(jnp.int32, (size, 1), 0)
                place = lax.broadcasted_iota(jnp.int32, (1, columns), 1) % block
                allowed = (key ^ turn) <= me * block + (place ^ turn)
            tile_of_heads(
                heads,
                lambda g: dot_turned(k_all[g, pl.ds(row, size), :], q_ref[g]),
                lambda g: v_all[g, :, pl.ds(row, size)],
                allowed,
                m_ref,
                acc_ref,
                False,
            )

        tile(last, True)

        def one(j, _):
            tile(j, False)
            return 0

        lax.fori_loop(0, last, one, 0)
        for g in range(heads):
            mixed = acc_ref[g, :HEAD_DIM, :] / acc_ref[g, HEAD_DIM : HEAD_DIM + 1, :]
            mixed = mixed.T.astype(jnp.bfloat16)
            for e in range(GROUPING):
                for r in range(planes):
                    at = e * block + r * rows
                    h = g * GROUPING + e
                    o_refs[r][:, h * HEAD_DIM : (h + 1) * HEAD_DIM] = mixed[at : at + rows]

    out = jax.ShapeDtypeStruct((rows, heads * GROUPING * HEAD_DIM), jnp.bfloat16)
    return pl.pallas_call(
        kernel,
        out_shape=[out] * planes,
        in_specs=[in_vmem()] * (3 + len(flat)),
        out_specs=[in_vmem()] * planes,
        scratch_shapes=[
            pltpu.VMEM(m.shape, jnp.float32),
            pltpu.VMEM(acc.shape, jnp.float32),
            pltpu.VMEM((heads, tokens, HEAD_DIM), jnp.bfloat16),
            pltpu.VMEM((heads, V_ROWS, tokens), jnp.bfloat16),
        ],
        compiler_params=params(),
        cost_estimate=pl.CostEstimate(
            flops=4 * heads * columns * tokens * HEAD_DIM, bytes_accessed=2**22,
            transcendentals=heads * columns * tokens
        ),
        name="attend_span",
    )(q_all, m, acc, *flat)


def swapped(shard, axis, bits):
    return lax.ppermute(shard, axis, [(i, i ^ bits) for i in range(lax.axis_size(axis))])


def gathered_shards(queries, keys, values, prefix_keys, prefix_values, span_start):
    planes = lax.axis_size("head")
    blocks = lax.axis_size("seq")
    kv, q = split_planes(queries, keys, values)
    kv = [kv[0]] + [swapped(kv[r], "head", r) for r in range(1, planes)]
    q = [q[0]] + [swapped(q[r], "head", r) for r in range(1, planes)]
    turned = turn_prefix_values(prefix_values)
    halves = [stack_pair(kv[r], kv[r + 1]) for r in range(0, planes, 2)]
    near = [halves] + [[swapped(h, "seq", c) for h in halves] for c in range(2, blocks, 2)]
    far = [[swapped(h, "seq", 1) for h in source] for source in near]
    sources = [source for couple in zip(near, far) for source in couple]
    q_all, m, acc = attend_prefix(span_start, q, prefix_keys, turned)
    pieces = attend_span(q_all, m, acc, sources)
    pieces = [pieces[0]] + [swapped(pieces[r], "head", r) for r in range(1, planes)]
    return join_planes(pieces)


def solution(mesh):
    placed = (
        P(("seq", "head"), None),
        P(("seq", "head"), None),
        P(("seq", "head"), None),
        P(None, "head"),
        P(None, "head"),
        P(),
    )
    fits = mesh.shape["seq"] == 8 and mesh.shape["head"] == 4
    shards = gathered_shards if fits else relayed_shards
    return jax.shard_map(
        shards, mesh=mesh, in_specs=placed, out_specs=P(("seq", "head"), None), check_vma=False
    )
```

```python
import jax
import jax.numpy as jnp
from jax import lax
from jax.experimental import pallas as pl
from jax.experimental.pallas import tpu as pltpu
from jax.sharding import PartitionSpec as P

HEAD_DIM = 128
QH = 32
KVH = 16
QSCALE = 144
WINDOW = 4096
EXP2_SCALE = 1.4426950408889634 * QSCALE**-0.5
LOWEST = -1e30
ONES_ROWS = 16
V_ROWS = HEAD_DIM + ONES_ROWS
TILE = 512
BOTH = ("seq", "head")


def shifted(shard, axis, by):
    size = lax.axis_size(axis)
    pairs = [(i, i + by) for i in range(size) if 0 <= i + by < size]
    return lax.ppermute(shard, axis, pairs)


def shortened(shard):
    return jax.tree.map(lambda a: a.astype(jnp.bfloat16) if a.dtype == jnp.float32 else a, shard)


def attend_block(query_rows, key_rows, value_rows, query_first, key_first, start_value):
    block_rows = query_rows.shape[0]
    key_count = key_rows.shape[0]
    grouping = QH // KVH
    scaling = QSCALE ** (-0.5)
    local_groups = key_rows.shape[1] // HEAD_DIM
    query_pos = query_first + jnp.arange(block_rows, dtype=jnp.int32)
    key_pos = key_first + jnp.arange(key_count, dtype=jnp.int32)
    distance = query_pos[:, None] - key_pos[None, :]
    allowed = (distance >= 0) & (distance < WINDOW) & (start_value + key_pos >= 0)[None, :]
    outputs = []
    for key_group in range(local_groups):
        lower = key_group * grouping * HEAD_DIM
        query_head = query_rows[:, lower : lower + grouping * HEAD_DIM].reshape(
            block_rows, grouping, HEAD_DIM
        )
        key_head = key_rows[:, key_group * HEAD_DIM : (key_group + 1) * HEAD_DIM]
        value_head = value_rows[:, key_group * HEAD_DIM : (key_group + 1) * HEAD_DIM]
        scores = (
            jnp.einsum("qgd,kd->gqk", query_head, key_head, preferred_element_type=jnp.float32)
            * scaling
        )
        scores = jnp.where(allowed[None], scores, -jnp.inf)
        peak_score = jnp.max(scores, axis=2, keepdims=True)
        unnormed = jnp.exp(scores - peak_score)
        totals = jnp.sum(unnormed, axis=2)
        weights = unnormed.astype(jnp.bfloat16)
        mixture = jnp.einsum("gqk,kd->qgd", weights, value_head, preferred_element_type=jnp.float32)
        outputs.append(
            (mixture / jnp.transpose(totals)[:, :, None]).reshape(block_rows, grouping * HEAD_DIM)
        )
    return jnp.concatenate(outputs, axis=1).astype(jnp.bfloat16)


def relayed_shards(queries, keys, values, prefix_keys, prefix_values, span_start):
    query_local, key_local, value_local = (
        lax.all_to_all(queries, "head", split_axis=1, concat_axis=0, tiled=True),
        lax.all_to_all(keys, "head", split_axis=1, concat_axis=0, tiled=True),
        lax.all_to_all(values, "head", split_axis=1, concat_axis=0, tiled=True),
    )
    seq_rows = query_local.shape[0]
    shards_back = WINDOW // seq_rows
    seq_index = lax.axis_index("seq")

    def relay(step, carried):
        moving_keys, moving_values, window_keys, window_values = carried
        moving_keys, moving_values = shifted((moving_keys, moving_values), "seq", 1)
        offset = (shards_back - 1 - step) * seq_rows
        window_keys = lax.dynamic_update_slice_in_dim(window_keys, moving_keys, offset, 0)
        window_values = lax.dynamic_update_slice_in_dim(window_values, moving_values, offset, 0)
        return (moving_keys, moving_values, window_keys, window_values)

    empty = jnp.zeros((WINDOW, key_local.shape[1]), jnp.bfloat16)
    carried = lax.fori_loop(0, shards_back, relay, (key_local, value_local, empty, empty))
    window_keys = carried[2]
    window_values = carried[3]
    first_row = jnp.minimum(seq_index * seq_rows, WINDOW)
    padded_keys = jnp.concatenate([prefix_keys, jnp.zeros_like(prefix_keys)], axis=0)
    padded_values = jnp.concatenate([prefix_values, jnp.zeros_like(prefix_values)], axis=0)
    window_keys = window_keys + lax.dynamic_slice_in_dim(padded_keys, first_row, WINDOW, 0)
    window_values = window_values + lax.dynamic_slice_in_dim(padded_values, first_row, WINDOW, 0)
    all_keys = jnp.concatenate([window_keys, key_local], axis=0)
    all_values = jnp.concatenate([window_values, value_local], axis=0)
    block_rows = min(512, seq_rows)
    block_count = seq_rows // block_rows
    start_value = span_start[0]
    key_base = (seq_index - shards_back) * seq_rows
    query_base = seq_index * seq_rows

    def one_block(block_index):
        first = block_index * block_rows
        return attend_block(
            query_local, all_keys, all_values, query_base + first, key_base + first, start_value
        )

    blocks = lax.map(one_block, jnp.arange(block_count, dtype=jnp.int32))
    attended = blocks.reshape(seq_rows, query_local.shape[1])
    return lax.all_to_all(
        shortened(attended), "head", split_axis=0, concat_axis=1, tiled=True
    ).astype(attended.dtype)


def in_vmem():
    return pl.BlockSpec(memory_space=pltpu.VMEM)


def in_smem():
    return pl.BlockSpec(memory_space=pltpu.SMEM)


def in_hbm():
    return pl.BlockSpec(memory_space=pltpu.HBM)


def params():
    return pltpu.CompilerParams(vmem_limit_bytes=32 * 2**20)


def cost(flops, moved):
    return pl.CostEstimate(flops=flops, bytes_accessed=moved, transcendentals=flops // 512)


def columns_of(head):
    return slice(head * HEAD_DIM, (head + 1) * HEAD_DIM)


def pack_heads(queries, keys, values, seq_size, head_size):
    rows = queries.shape[0]
    pairs = seq_size // 2

    def kernel(q_hbm, k_hbm, v_hbm, out_ref, q_ref, k_ref, v_ref, sems):
        copies = [
            pltpu.make_async_copy(source, target, sems.at[n])
            for n, (source, target) in enumerate(((q_hbm, q_ref), (k_hbm, k_ref), (v_hbm, v_ref)))
        ]
        for copy in copies:
            copy.start()
        copies[0].wait()
        for s in range(seq_size):
            for h in range(head_size):
                out_ref[s * head_size + h, :, :HEAD_DIM] = q_ref[:, columns_of(h * seq_size + s)]
        for parity, ref in ((0, k_ref), (1, v_ref)):
            copies[1 + parity].wait()
            for s in range(parity, seq_size, 2):
                for h in range(head_size):
                    out_ref[s * head_size + h, :, HEAD_DIM:] = ref[:, columns_of(h * pairs + s // 2)]

    return pl.pallas_call(
        kernel,
        out_shape=jax.ShapeDtypeStruct((seq_size * head_size, rows, 2 * HEAD_DIM), jnp.bfloat16),
        in_specs=[in_hbm()] * 3,
        out_specs=in_vmem(),
        scratch_shapes=[
            pltpu.VMEM(queries.shape, jnp.bfloat16),
            pltpu.VMEM(keys.shape, jnp.bfloat16),
            pltpu.VMEM(values.shape, jnp.bfloat16),
            pltpu.SemaphoreType.DMA((3,)),
        ],
        compiler_params=params(),
        cost_estimate=cost(0, 2**21),
        name="pack_heads",
    )(queries, keys, values)


def unpack_heads(chunks, seq_size, head_size):
    rows = chunks.shape[1]

    def kernel(in_ref, out_hbm, sems):
        copies = []
        for s in range(seq_size):
            for h in range(head_size):
                n = s * head_size + h
                copies.append(
                    pltpu.make_async_copy(
                        in_ref.at[n], out_hbm.at[:, columns_of(h * seq_size + s)], sems.at[n]
                    )
                )
        for copy in copies:
            copy.start()
        for copy in copies:
            copy.wait()

    return pl.pallas_call(
        kernel,
        out_shape=jax.ShapeDtypeStruct((rows, chunks.shape[0] * HEAD_DIM), jnp.bfloat16),
        in_specs=[in_vmem()],
        out_specs=in_hbm(),
        scratch_shapes=[pltpu.SemaphoreType.DMA((chunks.shape[0],))],
        compiler_params=params(),
        name="unpack_heads",
    )(chunks)


def prefix_of_head(prefix_keys, prefix_values):
    window = prefix_keys.shape[0]
    part = window // 4

    def kernel(k_hbm, v_hbm, k_ref, v_ref, held, sems):
        at = pl.ds(pl.multiple_of(lax.axis_index("seq") // 2 * HEAD_DIM, HEAD_DIM), HEAD_DIM)
        copies = [
            pltpu.make_async_copy(
                v_hbm.at[pl.ds(n * part, part), at], held.at[pl.ds(n * part, part)], sems.at[n]
            )
            for n in range(4)
        ]
        copies.append(pltpu.make_async_copy(k_hbm.at[:, at], k_ref, sems.at[4]))
        for copy in copies:
            copy.start()
        v_ref[HEAD_DIM:, :] = jnp.ones((ONES_ROWS, window), jnp.bfloat16)
        for n in range(4):
            copies[n].wait()
            v_ref[:HEAD_DIM, n * part : (n + 1) * part] = held[n * part : (n + 1) * part, :].T
        copies[4].wait()

    return pl.pallas_call(
        kernel,
        out_shape=[
            jax.ShapeDtypeStruct((window, HEAD_DIM), jnp.bfloat16),
            jax.ShapeDtypeStruct((V_ROWS, window), jnp.bfloat16),
        ],
        in_specs=[in_hbm()] * 2,
        out_specs=[in_vmem()] * 2,
        scratch_shapes=[
            pltpu.VMEM((window, HEAD_DIM), jnp.bfloat16),
            pltpu.SemaphoreType.DMA((5,)),
        ],
        compiler_params=params(),
        cost_estimate=cost(0, 2**23),
        name="prefix_of_head",
    )(prefix_keys, prefix_values)


def dot_turned(keys, queries):
    return lax.dot_general(
        keys, queries, (((1,), (1,)), ((), ())), preferred_element_type=jnp.float32
    )


def score_tile(keys, queries, allowed, s_ref, peak_ref):
    scores = dot_turned(keys, queries)
    if allowed is not None:
        scores = jnp.where(allowed, scores, -jnp.inf)
    s_ref[...] = scores
    return jnp.max(scores.reshape(scores.shape[0] // 8, 8, scores.shape[1]), axis=0)


def weigh_tile(s_ref, peak_ref, values, b, m_ref, acc_ref, following):
    before = m_ref[b, :1, :]
    peak = jnp.maximum(jnp.max(peak_ref[...], axis=0, keepdims=True), before)
    scaled = peak * EXP2_SCALE
    following_peak = following()
    weights = jnp.exp2(s_ref[...] * EXP2_SCALE - scaled).astype(jnp.bfloat16)
    sums = jnp.dot(values, weights, preferred_element_type=jnp.float32)
    if following_peak is not None:
        peak_ref[...] = following_peak
    acc_ref[b] = sums + acc_ref[b] * jnp.exp2(before * EXP2_SCALE - scaled)
    m_ref[b] = jnp.broadcast_to(peak, m_ref.shape[1:])


def attend_prefix(span_start, got, prefix_keys, prefix_values):
    tokens, window = got.shape[0], prefix_keys.shape[0]
    blocks = tokens // TILE

    def kernel(start_ref, q_ref, k_ref, v_ref, m_ref, acc_ref, s_a, s_b, peak_ref):
        first_key = window - start_ref[0]
        m_ref[...] = jnp.full(m_ref.shape, LOWEST, jnp.float32)
        acc_ref[...] = jnp.zeros(acc_ref.shape, jnp.float32)
        opening = [
            jnp.minimum(jnp.maximum(b * TILE + 1, first_key) // TILE, window // TILE - 1)
            for b in range(blocks)
        ]
        ends = []
        for b in range(blocks):
            count = window // TILE - 1 - opening[b]
            ends.append(count if b == 0 else ends[-1] + count)

        def place(i):
            b = sum((i >= end).astype(jnp.int32) for end in ends)
            tile = jnp.int32(0)
            for n in range(blocks):
                start = 0 if n == 0 else ends[n - 1]
                tile = jnp.where(b == n, opening[n] + 1 + i - start, tile)
            return b, pl.multiple_of(tile * TILE, TILE)

        def score(b, row, s_ref, allowed=None):
            at = pl.ds(pl.multiple_of(jnp.minimum(b, blocks - 1) * TILE, TILE), TILE)
            return score_tile(
                k_ref[pl.ds(row, TILE), :], q_ref[at, :HEAD_DIM], allowed, s_ref, peak_ref
            )

        def score_opening(b, s_ref):
            row = pl.multiple_of(opening[b] * TILE, TILE)
            key = lax.broadcasted_iota(jnp.int32, (TILE, TILE), 0)
            query = lax.broadcasted_iota(jnp.int32, (1, TILE), 1) + b * TILE
            allowed = key >= jnp.maximum(query + 1, first_key) - row
            return score(b, row, s_ref, allowed)

        def weigh(b, row, s_ref, following):
            weigh_tile(
                s_ref, peak_ref, v_ref[:, pl.ds(row, TILE)], b, m_ref, acc_ref, following
            )

        bufs = (s_a, s_b)
        peak_ref[...] = score_opening(0, s_a)
        for b in range(blocks):
            now, later = bufs[b % 2], bufs[(b + 1) % 2]
            if b + 1 < blocks:
                following = lambda b=b, later=later: score_opening(b + 1, later)
            else:
                following = lambda later=later: score(*place(jnp.int32(0)), later)
            weigh(b, pl.multiple_of(opening[b] * TILE, TILE), now, following)
        now, later = bufs[blocks % 2], bufs[(blocks + 1) % 2]

        def two(i, _):
            weigh(*place(2 * i), now, lambda: score(*place(2 * i + 1), later))
            weigh(*place(2 * i + 1), later, lambda: score(*place(2 * i + 2), now))
            return 0

        lax.fori_loop(0, (ends[-1] + 1) // 2, two, 0)

    return pl.pallas_call(
        kernel,
        out_shape=[
            jax.ShapeDtypeStruct((blocks + 1, 8, TILE), jnp.float32),
            jax.ShapeDtypeStruct((blocks + 1, V_ROWS, TILE), jnp.float32),
        ],
        in_specs=[in_smem()] + [in_vmem()] * 3,
        out_specs=[in_vmem()] * 2,
        scratch_shapes=[
            pltpu.VMEM((TILE, TILE), jnp.float32),
            pltpu.VMEM((TILE, TILE), jnp.float32),
            pltpu.VMEM((8, TILE), jnp.float32),
        ],
        compiler_params=params(),
        cost_estimate=cost(4 * tokens * window * HEAD_DIM, 2**22),
        name="attend_prefix",
    )(span_start, got, prefix_keys, prefix_values)


def attend_span(got, other, m, acc):
    tokens = got.shape[0]
    blocks = tokens // TILE

    def kernel(got_ref, other_ref, m_in, acc_in, o_ref, m_ref, acc_ref, k_ref, v_ref, s_a, s_b, peak_ref):
        holds_values = lax.axis_index("seq") % 2
        v_ref[HEAD_DIM:, :] = jnp.ones((ONES_ROWS, tokens), jnp.bfloat16)

        @pl.when(holds_values == 0)
        def _():
            k_ref[...] = got_ref[:, HEAD_DIM:]
            v_ref[:HEAD_DIM, :] = other_ref[...].T

        @pl.when(holds_values == 1)
        def _():
            k_ref[...] = other_ref[...]
            v_ref[:HEAD_DIM, :] = got_ref[:, HEAD_DIM:].T

        m_ref[...] = m_in[...]
        acc_ref[...] = acc_in[...]
        tiles = [(b, b) for b in range(blocks)]
        tiles += [(b, j) for b in range(blocks) for j in range(b)]

        def score(n, s_ref):
            b, j = tiles[n]
            allowed = None
            if b == j:
                key = lax.broadcasted_iota(jnp.int32, (TILE, TILE), 0)
                query = lax.broadcasted_iota(jnp.int32, (TILE, TILE), 1)
                allowed = key <= query
            return score_tile(
                k_ref[j * TILE : (j + 1) * TILE, :],
                got_ref[b * TILE : (b + 1) * TILE, :HEAD_DIM],
                allowed,
                s_ref,
                peak_ref,
            )

        bufs = (s_a, s_b)
        peak_ref[...] = score(0, s_a)
        for n, (b, j) in enumerate(tiles):
            more = n + 1 < len(tiles)
            weigh_tile(
                bufs[n % 2],
                peak_ref,
                v_ref[:, j * TILE : (j + 1) * TILE],
                b,
                m_ref,
                acc_ref,
                lambda n=n, more=more: score(n + 1, bufs[(n + 1) % 2]) if more else None,
            )
        for b in range(blocks):
            mixed = acc_ref[b, :HEAD_DIM, :] / acc_ref[b, HEAD_DIM : HEAD_DIM + 1, :]
            o_ref[b * TILE : (b + 1) * TILE, :] = mixed.T.astype(jnp.bfloat16)

    return pl.pallas_call(
        kernel,
        out_shape=jax.ShapeDtypeStruct((tokens, HEAD_DIM), jnp.bfloat16),
        in_specs=[in_vmem()] * 4,
        out_specs=in_vmem(),
        scratch_shapes=[
            pltpu.VMEM(m.shape, jnp.float32),
            pltpu.VMEM(acc.shape, jnp.float32),
            pltpu.VMEM((tokens, HEAD_DIM), jnp.bfloat16),
            pltpu.VMEM((V_ROWS, tokens), jnp.bfloat16),
            pltpu.VMEM((TILE, TILE), jnp.float32),
            pltpu.VMEM((TILE, TILE), jnp.float32),
            pltpu.VMEM((8, TILE), jnp.float32),
        ],
        compiler_params=params(),
        cost_estimate=cost(2 * tokens * tokens * HEAD_DIM, 2**22),
        name="attend_span",
    )(got, other, m, acc)


def spread_shards(queries, keys, values, prefix_keys, prefix_values, span_start):
    rows = queries.shape[0]
    seq_size, head_size = lax.axis_size("seq"), lax.axis_size("head")
    tokens = seq_size * head_size * rows
    packed = pack_heads(queries, keys, values, seq_size, head_size)
    got = lax.all_to_all(packed, BOTH, split_axis=0, concat_axis=0, tiled=True)
    got = got.reshape(tokens, 2 * HEAD_DIM)
    other = lax.ppermute(got[:, HEAD_DIM:], "seq", [(i, i ^ 1) for i in range(seq_size)])
    head_keys, head_values = prefix_of_head(prefix_keys, prefix_values)
    m, acc = attend_prefix(span_start, got, head_keys, head_values)
    attended = attend_span(got, other, m, acc)
    attended = attended.reshape(seq_size * head_size, rows, HEAD_DIM)
    back = lax.all_to_all(attended, BOTH, split_axis=0, concat_axis=0, tiled=True)
    return unpack_heads(back, seq_size, head_size)


def solution(mesh):
    placed = (
        P(("seq", "head"), None),
        P(("seq", "head"), None),
        P(("seq", "head"), None),
        P(None, "head"),
        P(None, "head"),
        P(),
    )
    fits = mesh.shape["seq"] * mesh.shape["head"] == QH and QH == 2 * KVH
    shards = spread_shards if fits else relayed_shards
    return jax.shard_map(
        shards, mesh=mesh, in_specs=placed, out_specs=P(("seq", "head"), None), check_vma=False
    )
```

```python
import jax
import jax.numpy as jnp
from jax import lax
from jax.experimental import pallas as pl
from jax.experimental.pallas import tpu as pltpu
from jax.sharding import PartitionSpec as P

HEAD_DIM = 128
QH = 32
KVH = 16
QSCALE = 144
WINDOW = 4096
EXP2_SCALE = 1.4426950408889634 * QSCALE**-0.5
LOWEST = -1e30
ONES_ROWS = 16
V_ROWS = HEAD_DIM + ONES_ROWS
TILE = 512
BOTH = ("seq", "head")


def shifted(shard, axis, by):
    size = lax.axis_size(axis)
    pairs = [(i, i + by) for i in range(size) if 0 <= i + by < size]
    return lax.ppermute(shard, axis, pairs)


def shortened(shard):
    return jax.tree.map(lambda a: a.astype(jnp.bfloat16) if a.dtype == jnp.float32 else a, shard)


def attend_block(query_rows, key_rows, value_rows, query_first, key_first, start_value):
    block_rows = query_rows.shape[0]
    key_count = key_rows.shape[0]
    grouping = QH // KVH
    scaling = QSCALE ** (-0.5)
    local_groups = key_rows.shape[1] // HEAD_DIM
    query_pos = query_first + jnp.arange(block_rows, dtype=jnp.int32)
    key_pos = key_first + jnp.arange(key_count, dtype=jnp.int32)
    distance = query_pos[:, None] - key_pos[None, :]
    allowed = (distance >= 0) & (distance < WINDOW) & (start_value + key_pos >= 0)[None, :]
    outputs = []
    for key_group in range(local_groups):
        lower = key_group * grouping * HEAD_DIM
        query_head = query_rows[:, lower : lower + grouping * HEAD_DIM].reshape(
            block_rows, grouping, HEAD_DIM
        )
        key_head = key_rows[:, key_group * HEAD_DIM : (key_group + 1) * HEAD_DIM]
        value_head = value_rows[:, key_group * HEAD_DIM : (key_group + 1) * HEAD_DIM]
        scores = (
            jnp.einsum("qgd,kd->gqk", query_head, key_head, preferred_element_type=jnp.float32)
            * scaling
        )
        scores = jnp.where(allowed[None], scores, -jnp.inf)
        peak_score = jnp.max(scores, axis=2, keepdims=True)
        unnormed = jnp.exp(scores - peak_score)
        totals = jnp.sum(unnormed, axis=2)
        weights = unnormed.astype(jnp.bfloat16)
        mixture = jnp.einsum("gqk,kd->qgd", weights, value_head, preferred_element_type=jnp.float32)
        outputs.append(
            (mixture / jnp.transpose(totals)[:, :, None]).reshape(block_rows, grouping * HEAD_DIM)
        )
    return jnp.concatenate(outputs, axis=1).astype(jnp.bfloat16)


def relayed_shards(queries, keys, values, prefix_keys, prefix_values, span_start):
    query_local, key_local, value_local = (
        lax.all_to_all(queries, "head", split_axis=1, concat_axis=0, tiled=True),
        lax.all_to_all(keys, "head", split_axis=1, concat_axis=0, tiled=True),
        lax.all_to_all(values, "head", split_axis=1, concat_axis=0, tiled=True),
    )
    seq_rows = query_local.shape[0]
    shards_back = WINDOW // seq_rows
    seq_index = lax.axis_index("seq")

    def relay(step, carried):
        moving_keys, moving_values, window_keys, window_values = carried
        moving_keys, moving_values = shifted((moving_keys, moving_values), "seq", 1)
        offset = (shards_back - 1 - step) * seq_rows
        window_keys = lax.dynamic_update_slice_in_dim(window_keys, moving_keys, offset, 0)
        window_values = lax.dynamic_update_slice_in_dim(window_values, moving_values, offset, 0)
        return (moving_keys, moving_values, window_keys, window_values)

    empty = jnp.zeros((WINDOW, key_local.shape[1]), jnp.bfloat16)
    carried = lax.fori_loop(0, shards_back, relay, (key_local, value_local, empty, empty))
    window_keys = carried[2]
    window_values = carried[3]
    first_row = jnp.minimum(seq_index * seq_rows, WINDOW)
    padded_keys = jnp.concatenate([prefix_keys, jnp.zeros_like(prefix_keys)], axis=0)
    padded_values = jnp.concatenate([prefix_values, jnp.zeros_like(prefix_values)], axis=0)
    window_keys = window_keys + lax.dynamic_slice_in_dim(padded_keys, first_row, WINDOW, 0)
    window_values = window_values + lax.dynamic_slice_in_dim(padded_values, first_row, WINDOW, 0)
    all_keys = jnp.concatenate([window_keys, key_local], axis=0)
    all_values = jnp.concatenate([window_values, value_local], axis=0)
    block_rows = min(512, seq_rows)
    block_count = seq_rows // block_rows
    start_value = span_start[0]
    key_base = (seq_index - shards_back) * seq_rows
    query_base = seq_index * seq_rows

    def one_block(block_index):
        first = block_index * block_rows
        return attend_block(
            query_local, all_keys, all_values, query_base + first, key_base + first, start_value
        )

    blocks = lax.map(one_block, jnp.arange(block_count, dtype=jnp.int32))
    attended = blocks.reshape(seq_rows, query_local.shape[1])
    return lax.all_to_all(
        shortened(attended), "head", split_axis=0, concat_axis=1, tiled=True
    ).astype(attended.dtype)


def in_vmem():
    return pl.BlockSpec(memory_space=pltpu.VMEM)


def in_smem():
    return pl.BlockSpec(memory_space=pltpu.SMEM)


def in_hbm():
    return pl.BlockSpec(memory_space=pltpu.HBM)


def params(mib=32):
    return pltpu.CompilerParams(vmem_limit_bytes=mib * 2**20)


def cost(flops, moved):
    return pl.CostEstimate(flops=flops, bytes_accessed=moved, transcendentals=flops // 512)


def columns_of(head):
    return slice(head * HEAD_DIM, (head + 1) * HEAD_DIM)


def pack_heads(queries, keys, values, seq_size, head_size):
    rows = queries.shape[0]
    pairs = seq_size // 2

    def kernel(q_hbm, k_hbm, v_hbm, out_ref, q_ref, k_ref, v_ref, sems):
        copies = [
            pltpu.make_async_copy(source, target, sems.at[n])
            for n, (source, target) in enumerate(((q_hbm, q_ref), (k_hbm, k_ref), (v_hbm, v_ref)))
        ]
        for copy in copies:
            copy.start()
        copies[0].wait()
        for s in range(seq_size):
            for h in range(head_size):
                out_ref[s * head_size + h, :, :HEAD_DIM] = q_ref[:, columns_of(h * seq_size + s)]
        for parity, ref in ((0, k_ref), (1, v_ref)):
            copies[1 + parity].wait()
            for s in range(parity, seq_size, 2):
                for h in range(head_size):
                    out_ref[s * head_size + h, :, HEAD_DIM:] = ref[:, columns_of(h * pairs + s // 2)]

    return pl.pallas_call(
        kernel,
        out_shape=jax.ShapeDtypeStruct((seq_size * head_size, rows, 2 * HEAD_DIM), jnp.bfloat16),
        in_specs=[in_hbm()] * 3,
        out_specs=in_vmem(),
        scratch_shapes=[
            pltpu.VMEM(queries.shape, jnp.bfloat16),
            pltpu.VMEM(keys.shape, jnp.bfloat16),
            pltpu.VMEM(values.shape, jnp.bfloat16),
            pltpu.SemaphoreType.DMA((3,)),
        ],
        compiler_params=params(62),
        cost_estimate=cost(0, 2**21),
        name="pack_heads",
    )(queries, keys, values)


def unpack_heads(chunks, seq_size, head_size):
    rows = chunks.shape[1]

    def kernel(in_ref, out_hbm, sems):
        copies = []
        for s in range(seq_size):
            for h in range(head_size):
                n = s * head_size + h
                copies.append(
                    pltpu.make_async_copy(
                        in_ref.at[n], out_hbm.at[:, columns_of(h * seq_size + s)], sems.at[n]
                    )
                )
        for copy in copies:
            copy.start()
        for copy in copies:
            copy.wait()

    return pl.pallas_call(
        kernel,
        out_shape=jax.ShapeDtypeStruct((rows, chunks.shape[0] * HEAD_DIM), jnp.bfloat16),
        in_specs=[in_vmem()],
        out_specs=in_hbm(),
        scratch_shapes=[pltpu.SemaphoreType.DMA((chunks.shape[0],))],
        compiler_params=params(),
        name="unpack_heads",
    )(chunks)


def prefix_of_head(prefix_keys, prefix_values):
    window = prefix_keys.shape[0]
    part = window // 4

    def kernel(k_hbm, v_hbm, k_ref, v_ref, held, sems):
        at = pl.ds(pl.multiple_of(lax.axis_index("seq") // 2 * HEAD_DIM, HEAD_DIM), HEAD_DIM)
        copies = [
            pltpu.make_async_copy(
                v_hbm.at[pl.ds(n * part, part), at], held.at[pl.ds(n * part, part)], sems.at[n]
            )
            for n in range(4)
        ]
        copies.append(pltpu.make_async_copy(k_hbm.at[:, at], k_ref, sems.at[4]))
        for copy in copies:
            copy.start()
        v_ref[HEAD_DIM:, :] = jnp.ones((ONES_ROWS, window), jnp.bfloat16)
        for n in range(4):
            copies[n].wait()
            v_ref[:HEAD_DIM, n * part : (n + 1) * part] = held[n * part : (n + 1) * part, :].T
        copies[4].wait()

    return pl.pallas_call(
        kernel,
        out_shape=[
            jax.ShapeDtypeStruct((window, HEAD_DIM), jnp.bfloat16),
            jax.ShapeDtypeStruct((V_ROWS, window), jnp.bfloat16),
        ],
        in_specs=[in_hbm()] * 2,
        out_specs=[in_vmem()] * 2,
        scratch_shapes=[
            pltpu.VMEM((window, HEAD_DIM), jnp.bfloat16),
            pltpu.SemaphoreType.DMA((5,)),
        ],
        compiler_params=params(32),
        cost_estimate=cost(0, 2**23),
        name="prefix_of_head",
    )(prefix_keys, prefix_values)


def dot_turned(keys, queries):
    return lax.dot_general(
        keys, queries, (((1,), (1,)), ((), ())), preferred_element_type=jnp.float32
    )


def score_tile(keys, queries, allowed, s_ref, peak_ref):
    scores = dot_turned(keys, queries)
    if allowed is not None:
        scores = jnp.where(allowed, scores, -jnp.inf)
    s_ref[...] = scores
    return jnp.max(scores.reshape(scores.shape[0] // 8, 8, scores.shape[1]), axis=0)


def weigh_tile(s_ref, peak_ref, values, b, m_ref, acc_ref, following):
    before = m_ref[b, :1, :]
    peak = jnp.maximum(jnp.max(peak_ref[...], axis=0, keepdims=True), before)
    scaled = peak * EXP2_SCALE
    following_peak = following()
    weights = jnp.exp2(s_ref[...] * EXP2_SCALE - scaled).astype(jnp.bfloat16)
    sums = jnp.dot(values, weights, preferred_element_type=jnp.float32)
    if following_peak is not None:
        peak_ref[...] = following_peak
    acc_ref[b] = sums + acc_ref[b] * jnp.exp2(before * EXP2_SCALE - scaled)
    m_ref[b] = jnp.broadcast_to(peak, m_ref.shape[1:])


def attend_prefix(span_start, got, prefix_keys, prefix_values):
    tokens, window = got.shape[0], prefix_keys.shape[0]
    blocks = tokens // TILE

    def kernel(start_ref, q_ref, k_ref, v_ref, m_ref, acc_ref, s_a, s_b, peak_ref):
        first_key = window - start_ref[0]
        m_ref[...] = jnp.full(m_ref.shape, LOWEST, jnp.float32)
        acc_ref[...] = jnp.zeros(acc_ref.shape, jnp.float32)
        opening = [
            jnp.minimum(jnp.maximum(b * TILE + 1, first_key) // TILE, window // TILE - 1)
            for b in range(blocks)
        ]
        ends = []
        for b in range(blocks):
            count = window // TILE - 1 - opening[b]
            ends.append(count if b == 0 else ends[-1] + count)

        def place(i):
            b = sum((i >= end).astype(jnp.int32) for end in ends)
            tile = jnp.int32(0)
            for n in range(blocks):
                start = 0 if n == 0 else ends[n - 1]
                tile = jnp.where(b == n, opening[n] + 1 + i - start, tile)
            return b, pl.multiple_of(tile * TILE, TILE)

        def score(b, row, s_ref, allowed=None):
            at = pl.ds(pl.multiple_of(jnp.minimum(b, blocks - 1) * TILE, TILE), TILE)
            return score_tile(
                k_ref[pl.ds(row, TILE), :], q_ref[at, :HEAD_DIM], allowed, s_ref, peak_ref
            )

        def score_opening(b, s_ref):
            row = pl.multiple_of(opening[b] * TILE, TILE)
            key = lax.broadcasted_iota(jnp.int32, (TILE, TILE), 0)
            query = lax.broadcasted_iota(jnp.int32, (1, TILE), 1) + b * TILE
            allowed = key >= jnp.maximum(query + 1, first_key) - row
            return score(b, row, s_ref, allowed)

        def weigh(b, row, s_ref, following):
            weigh_tile(
                s_ref, peak_ref, v_ref[:, pl.ds(row, TILE)], b, m_ref, acc_ref, following
            )

        bufs = (s_a, s_b)
        peak_ref[...] = score_opening(0, s_a)
        for b in range(blocks):
            now, later = bufs[b % 2], bufs[(b + 1) % 2]
            if b + 1 < blocks:
                following = lambda b=b, later=later: score_opening(b + 1, later)
            else:
                following = lambda later=later: score(*place(jnp.int32(0)), later)
            weigh(b, pl.multiple_of(opening[b] * TILE, TILE), now, following)
        now, later = bufs[blocks % 2], bufs[(blocks + 1) % 2]

        def two(i, _):
            weigh(*place(2 * i), now, lambda: score(*place(2 * i + 1), later))
            weigh(*place(2 * i + 1), later, lambda: score(*place(2 * i + 2), now))
            return 0

        lax.fori_loop(0, (ends[-1] + 1) // 2, two, 0)

    return pl.pallas_call(
        kernel,
        out_shape=[
            jax.ShapeDtypeStruct((blocks + 1, 8, TILE), jnp.float32),
            jax.ShapeDtypeStruct((blocks + 1, V_ROWS, TILE), jnp.float32),
        ],
        in_specs=[in_smem()] + [in_vmem()] * 3,
        out_specs=[in_vmem()] * 2,
        scratch_shapes=[
            pltpu.VMEM((TILE, TILE), jnp.float32),
            pltpu.VMEM((TILE, TILE), jnp.float32),
            pltpu.VMEM((8, TILE), jnp.float32),
        ],
        compiler_params=params(),
        cost_estimate=cost(4 * tokens * window * HEAD_DIM, 2**22),
        name="attend_prefix",
    )(span_start, got, prefix_keys, prefix_values)


def attend_span(got, other, m, acc):
    tokens = got.shape[0]
    blocks = tokens // TILE

    def kernel(got_ref, other_ref, m_in, acc_in, o_ref, m_ref, acc_ref, k_ref, v_ref, s_a, s_b, peak_ref):
        holds_values = lax.axis_index("seq") % 2
        v_ref[HEAD_DIM:, :] = jnp.ones((ONES_ROWS, tokens), jnp.bfloat16)

        @pl.when(holds_values == 0)
        def _():
            k_ref[...] = got_ref[:, HEAD_DIM:]
            v_ref[:HEAD_DIM, :] = other_ref[...].T

        @pl.when(holds_values == 1)
        def _():
            k_ref[...] = other_ref[...]
            v_ref[:HEAD_DIM, :] = got_ref[:, HEAD_DIM:].T

        m_ref[...] = m_in[...]
        acc_ref[...] = acc_in[...]
        tiles = [(b, b) for b in range(blocks)]
        tiles += [(b, j) for b in range(blocks) for j in range(b)]

        def score(n, s_ref):
            b, j = tiles[n]
            allowed = None
            if b == j:
                key = lax.broadcasted_iota(jnp.int32, (TILE, TILE), 0)
                query = lax.broadcasted_iota(jnp.int32, (TILE, TILE), 1)
                allowed = key <= query
            return score_tile(
                k_ref[j * TILE : (j + 1) * TILE, :],
                got_ref[b * TILE : (b + 1) * TILE, :HEAD_DIM],
                allowed,
                s_ref,
                peak_ref,
            )

        bufs = (s_a, s_b)
        peak_ref[...] = score(0, s_a)
        for n, (b, j) in enumerate(tiles):
            more = n + 1 < len(tiles)
            weigh_tile(
                bufs[n % 2],
                peak_ref,
                v_ref[:, j * TILE : (j + 1) * TILE],
                b,
                m_ref,
                acc_ref,
                lambda n=n, more=more: score(n + 1, bufs[(n + 1) % 2]) if more else None,
            )
        for b in range(blocks):
            mixed = acc_ref[b, :HEAD_DIM, :] / acc_ref[b, HEAD_DIM : HEAD_DIM + 1, :]
            o_ref[b * TILE : (b + 1) * TILE, :] = mixed.T.astype(jnp.bfloat16)

    return pl.pallas_call(
        kernel,
        out_shape=jax.ShapeDtypeStruct((tokens, HEAD_DIM), jnp.bfloat16),
        in_specs=[in_vmem()] * 4,
        out_specs=in_vmem(),
        scratch_shapes=[
            pltpu.VMEM(m.shape, jnp.float32),
            pltpu.VMEM(acc.shape, jnp.float32),
            pltpu.VMEM((tokens, HEAD_DIM), jnp.bfloat16),
            pltpu.VMEM((V_ROWS, tokens), jnp.bfloat16),
            pltpu.VMEM((TILE, TILE), jnp.float32),
            pltpu.VMEM((TILE, TILE), jnp.float32),
            pltpu.VMEM((8, TILE), jnp.float32),
        ],
        compiler_params=params(),
        cost_estimate=cost(2 * tokens * tokens * HEAD_DIM, 2**22),
        name="attend_span",
    )(got, other, m, acc)


def spread_shards(queries, keys, values, prefix_keys, prefix_values, span_start):
    rows = queries.shape[0]
    seq_size, head_size = lax.axis_size("seq"), lax.axis_size("head")
    tokens = seq_size * head_size * rows
    packed = pack_heads(queries, keys, values, seq_size, head_size)
    got = lax.all_to_all(packed, BOTH, split_axis=0, concat_axis=0, tiled=True)
    got = got.reshape(tokens, 2 * HEAD_DIM)
    head_keys, head_values = prefix_of_head(prefix_keys, prefix_values)
    got, head_keys, head_values = lax.optimization_barrier((got, head_keys, head_values))
    other = lax.ppermute(got[:, HEAD_DIM:], "seq", [(i, i ^ 1) for i in range(seq_size)])
    m, acc = attend_prefix(span_start, got, head_keys, head_values)
    attended = attend_span(got, other, m, acc)
    attended = attended.reshape(seq_size * head_size, rows, HEAD_DIM)
    back = lax.all_to_all(attended, BOTH, split_axis=0, concat_axis=0, tiled=True)
    return unpack_heads(back, seq_size, head_size)


def solution(mesh):
    placed = (
        P(("seq", "head"), None),
        P(("seq", "head"), None),
        P(("seq", "head"), None),
        P(None, "head"),
        P(None, "head"),
        P(),
    )
    fits = mesh.shape["seq"] * mesh.shape["head"] == QH and QH == 2 * KVH
    shards = spread_shards if fits else relayed_shards
    return jax.shard_map(
        shards, mesh=mesh, in_specs=placed, out_specs=P(("seq", "head"), None), check_vma=False
    )
```

```python
import jax
import jax.numpy as jnp
from jax import lax
from jax.experimental import pallas as pl
from jax.experimental.pallas import tpu as pltpu
from jax.sharding import PartitionSpec as P

HEAD_DIM = 128
QH = 32
KVH = 16
QSCALE = 144
WINDOW = 4096
EXP2_SCALE = 1.4426950408889634 * QSCALE**-0.5
LOWEST = -1e30
ONES_ROWS = 16
V_ROWS = HEAD_DIM + ONES_ROWS
TILE = 512
UNROLL = 6
BOTH = ("seq", "head")


def shifted(shard, axis, by):
    size = lax.axis_size(axis)
    pairs = [(i, i + by) for i in range(size) if 0 <= i + by < size]
    return lax.ppermute(shard, axis, pairs)


def shortened(shard):
    return jax.tree.map(lambda a: a.astype(jnp.bfloat16) if a.dtype == jnp.float32 else a, shard)


def attend_block(query_rows, key_rows, value_rows, query_first, key_first, start_value):
    block_rows = query_rows.shape[0]
    key_count = key_rows.shape[0]
    grouping = QH // KVH
    scaling = QSCALE ** (-0.5)
    local_groups = key_rows.shape[1] // HEAD_DIM
    query_pos = query_first + jnp.arange(block_rows, dtype=jnp.int32)
    key_pos = key_first + jnp.arange(key_count, dtype=jnp.int32)
    distance = query_pos[:, None] - key_pos[None, :]
    allowed = (distance >= 0) & (distance < WINDOW) & (start_value + key_pos >= 0)[None, :]
    outputs = []
    for key_group in range(local_groups):
        lower = key_group * grouping * HEAD_DIM
        query_head = query_rows[:, lower : lower + grouping * HEAD_DIM].reshape(
            block_rows, grouping, HEAD_DIM
        )
        key_head = key_rows[:, key_group * HEAD_DIM : (key_group + 1) * HEAD_DIM]
        value_head = value_rows[:, key_group * HEAD_DIM : (key_group + 1) * HEAD_DIM]
        scores = (
            jnp.einsum("qgd,kd->gqk", query_head, key_head, preferred_element_type=jnp.float32)
            * scaling
        )
        scores = jnp.where(allowed[None], scores, -jnp.inf)
        peak_score = jnp.max(scores, axis=2, keepdims=True)
        unnormed = jnp.exp(scores - peak_score)
        totals = jnp.sum(unnormed, axis=2)
        weights = unnormed.astype(jnp.bfloat16)
        mixture = jnp.einsum("gqk,kd->qgd", weights, value_head, preferred_element_type=jnp.float32)
        outputs.append(
            (mixture / jnp.transpose(totals)[:, :, None]).reshape(block_rows, grouping * HEAD_DIM)
        )
    return jnp.concatenate(outputs, axis=1).astype(jnp.bfloat16)


def relayed_shards(queries, keys, values, prefix_keys, prefix_values, span_start):
    query_local, key_local, value_local = (
        lax.all_to_all(queries, "head", split_axis=1, concat_axis=0, tiled=True),
        lax.all_to_all(keys, "head", split_axis=1, concat_axis=0, tiled=True),
        lax.all_to_all(values, "head", split_axis=1, concat_axis=0, tiled=True),
    )
    seq_rows = query_local.shape[0]
    shards_back = WINDOW // seq_rows
    seq_index = lax.axis_index("seq")

    def relay(step, carried):
        moving_keys, moving_values, window_keys, window_values = carried
        moving_keys, moving_values = shifted((moving_keys, moving_values), "seq", 1)
        offset = (shards_back - 1 - step) * seq_rows
        window_keys = lax.dynamic_update_slice_in_dim(window_keys, moving_keys, offset, 0)
        window_values = lax.dynamic_update_slice_in_dim(window_values, moving_values, offset, 0)
        return (moving_keys, moving_values, window_keys, window_values)

    empty = jnp.zeros((WINDOW, key_local.shape[1]), jnp.bfloat16)
    carried = lax.fori_loop(0, shards_back, relay, (key_local, value_local, empty, empty))
    window_keys = carried[2]
    window_values = carried[3]
    first_row = jnp.minimum(seq_index * seq_rows, WINDOW)
    padded_keys = jnp.concatenate([prefix_keys, jnp.zeros_like(prefix_keys)], axis=0)
    padded_values = jnp.concatenate([prefix_values, jnp.zeros_like(prefix_values)], axis=0)
    window_keys = window_keys + lax.dynamic_slice_in_dim(padded_keys, first_row, WINDOW, 0)
    window_values = window_values + lax.dynamic_slice_in_dim(padded_values, first_row, WINDOW, 0)
    all_keys = jnp.concatenate([window_keys, key_local], axis=0)
    all_values = jnp.concatenate([window_values, value_local], axis=0)
    block_rows = min(512, seq_rows)
    block_count = seq_rows // block_rows
    start_value = span_start[0]
    key_base = (seq_index - shards_back) * seq_rows
    query_base = seq_index * seq_rows

    def one_block(block_index):
        first = block_index * block_rows
        return attend_block(
            query_local, all_keys, all_values, query_base + first, key_base + first, start_value
        )

    blocks = lax.map(one_block, jnp.arange(block_count, dtype=jnp.int32))
    attended = blocks.reshape(seq_rows, query_local.shape[1])
    return lax.all_to_all(
        shortened(attended), "head", split_axis=0, concat_axis=1, tiled=True
    ).astype(attended.dtype)


def in_vmem():
    return pl.BlockSpec(memory_space=pltpu.VMEM)


def in_smem():
    return pl.BlockSpec(memory_space=pltpu.SMEM)


def in_hbm():
    return pl.BlockSpec(memory_space=pltpu.HBM)


def params(mib=32):
    return pltpu.CompilerParams(vmem_limit_bytes=mib * 2**20)


def cost(flops, moved):
    return pl.CostEstimate(flops=flops, bytes_accessed=moved, transcendentals=flops // 512)


def columns_of(head):
    return slice(head * HEAD_DIM, (head + 1) * HEAD_DIM)


def pack_heads(queries, keys, values, seq_size, head_size):
    rows = queries.shape[0]
    pairs = seq_size // 2

    def kernel(q_hbm, k_hbm, v_hbm, out_ref, q_ref, k_ref, v_ref, sems):
        copies = [
            pltpu.make_async_copy(source, target, sems.at[n])
            for n, (source, target) in enumerate(((q_hbm, q_ref), (k_hbm, k_ref), (v_hbm, v_ref)))
        ]
        for copy in copies:
            copy.start()
        copies[0].wait()
        for s in range(seq_size):
            for h in range(head_size):
                out_ref[s * head_size + h, :, :HEAD_DIM] = q_ref[:, columns_of(h * seq_size + s)]
        for parity, ref in ((0, k_ref), (1, v_ref)):
            copies[1 + parity].wait()
            for s in range(parity, seq_size, 2):
                for h in range(head_size):
                    out_ref[s * head_size + h, :, HEAD_DIM:] = ref[:, columns_of(h * pairs + s // 2)]

    return pl.pallas_call(
        kernel,
        out_shape=jax.ShapeDtypeStruct((seq_size * head_size, rows, 2 * HEAD_DIM), jnp.bfloat16),
        in_specs=[in_hbm()] * 3,
        out_specs=in_vmem(),
        scratch_shapes=[
            pltpu.VMEM(queries.shape, jnp.bfloat16),
            pltpu.VMEM(keys.shape, jnp.bfloat16),
            pltpu.VMEM(values.shape, jnp.bfloat16),
            pltpu.SemaphoreType.DMA((3,)),
        ],
        compiler_params=params(62),
        cost_estimate=cost(0, 2**21),
        name="pack_heads",
    )(queries, keys, values)


def unpack_heads(chunks, seq_size, head_size):
    rows = chunks.shape[1]

    def kernel(in_ref, out_hbm, sems):
        copies = []
        for s in range(seq_size):
            for h in range(head_size):
                n = s * head_size + h
                copies.append(
                    pltpu.make_async_copy(
                        in_ref.at[n], out_hbm.at[:, columns_of(h * seq_size + s)], sems.at[n]
                    )
                )
        for copy in copies:
            copy.start()
        for copy in copies:
            copy.wait()

    return pl.pallas_call(
        kernel,
        out_shape=jax.ShapeDtypeStruct((rows, chunks.shape[0] * HEAD_DIM), jnp.bfloat16),
        in_specs=[in_vmem()],
        out_specs=in_hbm(),
        scratch_shapes=[pltpu.SemaphoreType.DMA((chunks.shape[0],))],
        compiler_params=params(),
        name="unpack_heads",
    )(chunks)


def prefix_of_head(prefix_keys, prefix_values):
    window = prefix_keys.shape[0]
    part = window // 4

    def kernel(k_hbm, v_hbm, k_ref, v_ref, held, sems):
        at = pl.ds(pl.multiple_of(lax.axis_index("seq") // 2 * HEAD_DIM, HEAD_DIM), HEAD_DIM)
        copies = [
            pltpu.make_async_copy(
                v_hbm.at[pl.ds(n * part, part), at], held.at[pl.ds(n * part, part)], sems.at[n]
            )
            for n in range(4)
        ]
        copies.append(pltpu.make_async_copy(k_hbm.at[:, at], k_ref, sems.at[4]))
        for copy in copies:
            copy.start()
        v_ref[HEAD_DIM:, :] = jnp.ones((ONES_ROWS, window), jnp.bfloat16)
        for n in range(4):
            copies[n].wait()
            v_ref[:HEAD_DIM, n * part : (n + 1) * part] = held[n * part : (n + 1) * part, :].T
        copies[4].wait()

    return pl.pallas_call(
        kernel,
        out_shape=[
            jax.ShapeDtypeStruct((window, HEAD_DIM), jnp.bfloat16),
            jax.ShapeDtypeStruct((V_ROWS, window), jnp.bfloat16),
        ],
        in_specs=[in_hbm()] * 2,
        out_specs=[in_vmem()] * 2,
        scratch_shapes=[
            pltpu.VMEM((window, HEAD_DIM), jnp.bfloat16),
            pltpu.SemaphoreType.DMA((5,)),
        ],
        compiler_params=params(32),
        cost_estimate=cost(0, 2**23),
        name="prefix_of_head",
    )(prefix_keys, prefix_values)


def dot_turned(keys, queries):
    return lax.dot_general(
        keys, queries, (((1,), (1,)), ((), ())), preferred_element_type=jnp.float32
    )


def score_tile(keys, queries, allowed, s_ref, peak_ref):
    scores = dot_turned(keys, queries)
    if allowed is not None:
        scores = jnp.where(allowed, scores, -jnp.inf)
    s_ref[...] = scores
    return jnp.max(scores.reshape(scores.shape[0] // 8, 8, scores.shape[1]), axis=0)


def weigh_tile(s_ref, peak_ref, values, b, old, m_ref, acc_ref, following):
    old_m, old_acc = old
    before = old_m[b, :1, :]
    peak = jnp.maximum(jnp.max(peak_ref[...], axis=0, keepdims=True), before)
    scaled = peak * EXP2_SCALE
    following_peak = following()
    weights = jnp.exp2(s_ref[...] * EXP2_SCALE - scaled).astype(jnp.bfloat16)
    sums = jnp.dot(values, weights, preferred_element_type=jnp.float32)
    if following_peak is not None:
        peak_ref[...] = following_peak
    acc_ref[b] = sums + old_acc[b] * jnp.exp2(before * EXP2_SCALE - scaled)
    m_ref[b] = jnp.broadcast_to(peak, m_ref.shape[1:])


def attend_prefix(span_start, got, prefix_keys, prefix_values):
    tokens, window = got.shape[0], prefix_keys.shape[0]
    blocks = tokens // TILE

    def kernel(start_ref, q_ref, k_ref, v_ref, m_ref, acc_ref, s_a, s_b, peak_ref):
        first_key = window - start_ref[0]
        m_ref[...] = jnp.full(m_ref.shape, LOWEST, jnp.float32)
        acc_ref[...] = jnp.zeros(acc_ref.shape, jnp.float32)
        opening = [
            jnp.minimum(jnp.maximum(b * TILE + 1, first_key) // TILE, window // TILE - 1)
            for b in range(blocks)
        ]
        ends = []
        for b in range(blocks):
            count = window // TILE - 1 - opening[b]
            ends.append(count if b == 0 else ends[-1] + count)

        def place(i):
            b = sum((i >= end).astype(jnp.int32) for end in ends)
            tile = jnp.int32(0)
            for n in range(blocks):
                start = 0 if n == 0 else ends[n - 1]
                tile = jnp.where(b == n, opening[n] + 1 + i - start, tile)
            return b, pl.multiple_of(tile * TILE, TILE)

        def score(b, row, s_ref, allowed=None):
            at = pl.ds(pl.multiple_of(jnp.minimum(b, blocks - 1) * TILE, TILE), TILE)
            return score_tile(
                k_ref[pl.ds(row, TILE), :], q_ref[at, :HEAD_DIM], allowed, s_ref, peak_ref
            )

        def score_opening(b, s_ref):
            row = pl.multiple_of(opening[b] * TILE, TILE)
            key = lax.broadcasted_iota(jnp.int32, (TILE, TILE), 0)
            query = lax.broadcasted_iota(jnp.int32, (1, TILE), 1) + b * TILE
            allowed = key >= jnp.maximum(query + 1, first_key) - row
            return score(b, row, s_ref, allowed)

        def weigh(b, row, s_ref, following):
            weigh_tile(
                s_ref,
                peak_ref,
                v_ref[:, pl.ds(row, TILE)],
                b,
                (m_ref, acc_ref),
                m_ref,
                acc_ref,
                following,
            )

        bufs = (s_a, s_b)
        peak_ref[...] = score_opening(0, s_a)
        for b in range(blocks):
            now, later = bufs[b % 2], bufs[(b + 1) % 2]
            if b + 1 < blocks:
                following = lambda b=b, later=later: score_opening(b + 1, later)
            else:
                following = lambda later=later: score(*place(jnp.int32(0)), later)
            weigh(b, pl.multiple_of(opening[b] * TILE, TILE), now, following)
        now, later = bufs[blocks % 2], bufs[(blocks + 1) % 2]

        def several(first, count):
            for n in range(0, count, 2):
                i = first + n
                weigh(*place(i), now, lambda i=i: score(*place(i + 1), later))
                weigh(*place(i + 1), later, lambda i=i: score(*place(i + 2), now))

        many = ends[-1] // UNROLL

        def unrolled(i, _):
            several(i * UNROLL, UNROLL)
            return 0

        def rest(i, _):
            several(many * UNROLL + 2 * i, 2)
            return 0

        lax.fori_loop(0, many, unrolled, 0)
        lax.fori_loop(0, (ends[-1] - many * UNROLL + 1) // 2, rest, 0)

    return pl.pallas_call(
        kernel,
        out_shape=[
            jax.ShapeDtypeStruct((blocks + 1, 8, TILE), jnp.float32),
            jax.ShapeDtypeStruct((blocks + 1, V_ROWS, TILE), jnp.float32),
        ],
        in_specs=[in_smem()] + [in_vmem()] * 3,
        out_specs=[in_vmem()] * 2,
        scratch_shapes=[
            pltpu.VMEM((TILE, TILE), jnp.float32),
            pltpu.VMEM((TILE, TILE), jnp.float32),
            pltpu.VMEM((8, TILE), jnp.float32),
        ],
        compiler_params=params(),
        cost_estimate=cost(4 * tokens * window * HEAD_DIM, 2**22),
        name="attend_prefix",
    )(span_start, got, prefix_keys, prefix_values)


def attend_span(got, other, m, acc):
    tokens = got.shape[0]
    blocks = tokens // TILE

    def kernel(got_ref, other_ref, m_in, acc_in, o_ref, m_ref, acc_ref, k_ref, v_ref, held, s_a, s_b, peak_ref):
        holds_values = lax.axis_index("seq") % 2
        v_ref[HEAD_DIM:, :] = jnp.ones((ONES_ROWS, tokens), jnp.bfloat16)

        @pl.when(holds_values == 0)
        def _():
            k_ref[...] = got_ref[:, HEAD_DIM:]
            held[...] = other_ref[...]

        @pl.when(holds_values == 1)
        def _():
            k_ref[...] = other_ref[...]
            held[...] = got_ref[:, HEAD_DIM:]

        tiles = [(b, b) for b in range(blocks)]
        tiles += [(b, j) for b in range(blocks) for j in range(b)]

        def score(n, s_ref):
            b, j = tiles[n]
            allowed = None
            if b == j:
                key = lax.broadcasted_iota(jnp.int32, (TILE, TILE), 0)
                query = lax.broadcasted_iota(jnp.int32, (TILE, TILE), 1)
                allowed = key <= query
            return score_tile(
                k_ref[j * TILE : (j + 1) * TILE, :],
                got_ref[b * TILE : (b + 1) * TILE, :HEAD_DIM],
                allowed,
                s_ref,
                peak_ref,
            )

        bufs = (s_a, s_b)
        peak_ref[...] = score(0, s_a)
        for n, (b, j) in enumerate(tiles):
            more = n + 1 < len(tiles)
            at = slice(j * TILE, (j + 1) * TILE)
            if b == j:
                v_ref[:HEAD_DIM, at] = held[at, :].T
            weigh_tile(
                bufs[n % 2],
                peak_ref,
                v_ref[:, j * TILE : (j + 1) * TILE],
                b,
                (m_in, acc_in) if b == j else (m_ref, acc_ref),
                m_ref,
                acc_ref,
                lambda n=n, more=more: score(n + 1, bufs[(n + 1) % 2]) if more else None,
            )
        for b in range(blocks):
            mixed = acc_ref[b, :HEAD_DIM, :] / acc_ref[b, HEAD_DIM : HEAD_DIM + 1, :]
            o_ref[b * TILE : (b + 1) * TILE, :] = mixed.T.astype(jnp.bfloat16)

    return pl.pallas_call(
        kernel,
        out_shape=jax.ShapeDtypeStruct((tokens, HEAD_DIM), jnp.bfloat16),
        in_specs=[in_vmem()] * 4,
        out_specs=in_vmem(),
        scratch_shapes=[
            pltpu.VMEM(m.shape, jnp.float32),
            pltpu.VMEM(acc.shape, jnp.float32),
            pltpu.VMEM((tokens, HEAD_DIM), jnp.bfloat16),
            pltpu.VMEM((V_ROWS, tokens), jnp.bfloat16),
            pltpu.VMEM((tokens, HEAD_DIM), jnp.bfloat16),
            pltpu.VMEM((TILE, TILE), jnp.float32),
            pltpu.VMEM((TILE, TILE), jnp.float32),
            pltpu.VMEM((8, TILE), jnp.float32),
        ],
        compiler_params=params(),
        cost_estimate=cost(2 * tokens * tokens * HEAD_DIM, 2**22),
        name="attend_span",
    )(got, other, m, acc)


def spread_shards(queries, keys, values, prefix_keys, prefix_values, span_start):
    rows = queries.shape[0]
    seq_size, head_size = lax.axis_size("seq"), lax.axis_size("head")
    tokens = seq_size * head_size * rows
    packed = pack_heads(queries, keys, values, seq_size, head_size)
    got = lax.all_to_all(packed, BOTH, split_axis=0, concat_axis=0, tiled=True)
    got = got.reshape(tokens, 2 * HEAD_DIM)
    head_keys, head_values = prefix_of_head(prefix_keys, prefix_values)
    got, head_keys, head_values = lax.optimization_barrier((got, head_keys, head_values))
    other = lax.ppermute(got[:, HEAD_DIM:], "seq", [(i, i ^ 1) for i in range(seq_size)])
    m, acc = attend_prefix(span_start, got, head_keys, head_values)
    attended = attend_span(got, other, m, acc)
    attended = attended.reshape(seq_size * head_size, rows, HEAD_DIM)
    back = lax.all_to_all(attended, BOTH, split_axis=0, concat_axis=0, tiled=True)
    return unpack_heads(back, seq_size, head_size)


def solution(mesh):
    placed = (
        P(("seq", "head"), None),
        P(("seq", "head"), None),
        P(("seq", "head"), None),
        P(None, "head"),
        P(None, "head"),
        P(),
    )
    fits = mesh.shape["seq"] * mesh.shape["head"] == QH and QH == 2 * KVH
    shards = spread_shards if fits else relayed_shards
    return jax.shard_map(
        shards, mesh=mesh, in_specs=placed, out_specs=P(("seq", "head"), None), check_vma=False
    )
```

```python
import jax
import jax.numpy as jnp
from jax import lax
from jax.experimental import pallas as pl
from jax.experimental.pallas import tpu as pltpu
from jax.sharding import PartitionSpec as P

HEAD_DIM = 128
QH = 32
KVH = 16
QSCALE = 144
WINDOW = 4096
EXP2_SCALE = 1.4426950408889634 * QSCALE**-0.5
LOWEST = -1e30
ONES_ROWS = 16
V_ROWS = HEAD_DIM + ONES_ROWS
TILE = 512
UNROLL = 6
BOTH = ("seq", "head")


def shifted(shard, axis, by):
    size = lax.axis_size(axis)
    pairs = [(i, i + by) for i in range(size) if 0 <= i + by < size]
    return lax.ppermute(shard, axis, pairs)


def shortened(shard):
    return jax.tree.map(lambda a: a.astype(jnp.bfloat16) if a.dtype == jnp.float32 else a, shard)


def attend_block(query_rows, key_rows, value_rows, query_first, key_first, start_value):
    block_rows = query_rows.shape[0]
    key_count = key_rows.shape[0]
    grouping = QH // KVH
    scaling = QSCALE ** (-0.5)
    local_groups = key_rows.shape[1] // HEAD_DIM
    query_pos = query_first + jnp.arange(block_rows, dtype=jnp.int32)
    key_pos = key_first + jnp.arange(key_count, dtype=jnp.int32)
    distance = query_pos[:, None] - key_pos[None, :]
    allowed = (distance >= 0) & (distance < WINDOW) & (start_value + key_pos >= 0)[None, :]
    outputs = []
    for key_group in range(local_groups):
        lower = key_group * grouping * HEAD_DIM
        query_head = query_rows[:, lower : lower + grouping * HEAD_DIM].reshape(
            block_rows, grouping, HEAD_DIM
        )
        key_head = key_rows[:, key_group * HEAD_DIM : (key_group + 1) * HEAD_DIM]
        value_head = value_rows[:, key_group * HEAD_DIM : (key_group + 1) * HEAD_DIM]
        scores = (
            jnp.einsum("qgd,kd->gqk", query_head, key_head, preferred_element_type=jnp.float32)
            * scaling
        )
        scores = jnp.where(allowed[None], scores, -jnp.inf)
        peak_score = jnp.max(scores, axis=2, keepdims=True)
        unnormed = jnp.exp(scores - peak_score)
        totals = jnp.sum(unnormed, axis=2)
        weights = unnormed.astype(jnp.bfloat16)
        mixture = jnp.einsum("gqk,kd->qgd", weights, value_head, preferred_element_type=jnp.float32)
        outputs.append(
            (mixture / jnp.transpose(totals)[:, :, None]).reshape(block_rows, grouping * HEAD_DIM)
        )
    return jnp.concatenate(outputs, axis=1).astype(jnp.bfloat16)


def relayed_shards(queries, keys, values, prefix_keys, prefix_values, span_start):
    query_local, key_local, value_local = (
        lax.all_to_all(queries, "head", split_axis=1, concat_axis=0, tiled=True),
        lax.all_to_all(keys, "head", split_axis=1, concat_axis=0, tiled=True),
        lax.all_to_all(values, "head", split_axis=1, concat_axis=0, tiled=True),
    )
    seq_rows = query_local.shape[0]
    shards_back = WINDOW // seq_rows
    seq_index = lax.axis_index("seq")

    def relay(step, carried):
        moving_keys, moving_values, window_keys, window_values = carried
        moving_keys, moving_values = shifted((moving_keys, moving_values), "seq", 1)
        offset = (shards_back - 1 - step) * seq_rows
        window_keys = lax.dynamic_update_slice_in_dim(window_keys, moving_keys, offset, 0)
        window_values = lax.dynamic_update_slice_in_dim(window_values, moving_values, offset, 0)
        return (moving_keys, moving_values, window_keys, window_values)

    empty = jnp.zeros((WINDOW, key_local.shape[1]), jnp.bfloat16)
    carried = lax.fori_loop(0, shards_back, relay, (key_local, value_local, empty, empty))
    window_keys = carried[2]
    window_values = carried[3]
    first_row = jnp.minimum(seq_index * seq_rows, WINDOW)
    padded_keys = jnp.concatenate([prefix_keys, jnp.zeros_like(prefix_keys)], axis=0)
    padded_values = jnp.concatenate([prefix_values, jnp.zeros_like(prefix_values)], axis=0)
    window_keys = window_keys + lax.dynamic_slice_in_dim(padded_keys, first_row, WINDOW, 0)
    window_values = window_values + lax.dynamic_slice_in_dim(padded_values, first_row, WINDOW, 0)
    all_keys = jnp.concatenate([window_keys, key_local], axis=0)
    all_values = jnp.concatenate([window_values, value_local], axis=0)
    block_rows = min(512, seq_rows)
    block_count = seq_rows // block_rows
    start_value = span_start[0]
    key_base = (seq_index - shards_back) * seq_rows
    query_base = seq_index * seq_rows

    def one_block(block_index):
        first = block_index * block_rows
        return attend_block(
            query_local, all_keys, all_values, query_base + first, key_base + first, start_value
        )

    blocks = lax.map(one_block, jnp.arange(block_count, dtype=jnp.int32))
    attended = blocks.reshape(seq_rows, query_local.shape[1])
    return lax.all_to_all(
        shortened(attended), "head", split_axis=0, concat_axis=1, tiled=True
    ).astype(attended.dtype)


def in_vmem():
    return pl.BlockSpec(memory_space=pltpu.VMEM)


def in_smem():
    return pl.BlockSpec(memory_space=pltpu.SMEM)


def in_hbm():
    return pl.BlockSpec(memory_space=pltpu.HBM)


def params(mib=32):
    return pltpu.CompilerParams(vmem_limit_bytes=mib * 2**20)


def cost(flops, moved):
    return pl.CostEstimate(flops=flops, bytes_accessed=moved, transcendentals=flops // 512)


def columns_of(head):
    return slice(head * HEAD_DIM, (head + 1) * HEAD_DIM)


def pack_heads(queries, keys, values, seq_size, head_size):
    rows = queries.shape[0]
    pairs = seq_size // 2

    def kernel(q_hbm, k_hbm, v_hbm, out_ref, q_ref, k_ref, v_ref, sems):
        copies = [
            pltpu.make_async_copy(source, target, sems.at[n])
            for n, (source, target) in enumerate(((q_hbm, q_ref), (k_hbm, k_ref), (v_hbm, v_ref)))
        ]
        for copy in copies:
            copy.start()
        copies[0].wait()
        for s in range(seq_size):
            for h in range(head_size):
                out_ref[s * head_size + h, :, :HEAD_DIM] = q_ref[:, columns_of(h * seq_size + s)]
        for parity, ref in ((0, k_ref), (1, v_ref)):
            copies[1 + parity].wait()
            for s in range(parity, seq_size, 2):
                for h in range(head_size):
                    out_ref[s * head_size + h, :, HEAD_DIM:] = ref[:, columns_of(h * pairs + s // 2)]

    return pl.pallas_call(
        kernel,
        out_shape=jax.ShapeDtypeStruct((seq_size * head_size, rows, 2 * HEAD_DIM), jnp.bfloat16),
        in_specs=[in_hbm()] * 3,
        out_specs=in_vmem(),
        scratch_shapes=[
            pltpu.VMEM(queries.shape, jnp.bfloat16),
            pltpu.VMEM(keys.shape, jnp.bfloat16),
            pltpu.VMEM(values.shape, jnp.bfloat16),
            pltpu.SemaphoreType.DMA((3,)),
        ],
        compiler_params=params(62),
        cost_estimate=cost(0, 2**21),
        name="pack_heads",
    )(queries, keys, values)


def unpack_heads(chunks, seq_size, head_size):
    rows = chunks.shape[1]

    def kernel(in_ref, out_hbm, sems):
        copies = []
        for s in range(seq_size):
            for h in range(head_size):
                n = s * head_size + h
                copies.append(
                    pltpu.make_async_copy(
                        in_ref.at[n], out_hbm.at[:, columns_of(h * seq_size + s)], sems.at[n]
                    )
                )
        for copy in copies:
            copy.start()
        for copy in copies:
            copy.wait()

    return pl.pallas_call(
        kernel,
        out_shape=jax.ShapeDtypeStruct((rows, chunks.shape[0] * HEAD_DIM), jnp.bfloat16),
        in_specs=[in_vmem()],
        out_specs=in_hbm(),
        scratch_shapes=[pltpu.SemaphoreType.DMA((chunks.shape[0],))],
        compiler_params=params(),
        name="unpack_heads",
    )(chunks)


def prefix_of_head(prefix_keys, prefix_values):
    window = prefix_keys.shape[0]
    part = window // 4

    def kernel(k_hbm, v_hbm, k_ref, v_ref, held, sems):
        at = pl.ds(pl.multiple_of(lax.axis_index("seq") // 2 * HEAD_DIM, HEAD_DIM), HEAD_DIM)
        copies = [
            pltpu.make_async_copy(
                v_hbm.at[pl.ds(n * part, part), at], held.at[pl.ds(n * part, part)], sems.at[n]
            )
            for n in range(4)
        ]
        copies.append(pltpu.make_async_copy(k_hbm.at[:, at], k_ref, sems.at[4]))
        for copy in copies:
            copy.start()
        v_ref[HEAD_DIM:, :] = jnp.ones((ONES_ROWS, window), jnp.bfloat16)
        for n in range(4):
            copies[n].wait()
            v_ref[:HEAD_DIM, n * part : (n + 1) * part] = held[n * part : (n + 1) * part, :].T
        copies[4].wait()

    return pl.pallas_call(
        kernel,
        out_shape=[
            jax.ShapeDtypeStruct((window, HEAD_DIM), jnp.bfloat16),
            jax.ShapeDtypeStruct((V_ROWS, window), jnp.bfloat16),
        ],
        in_specs=[in_hbm()] * 2,
        out_specs=[in_vmem()] * 2,
        scratch_shapes=[
            pltpu.VMEM((window, HEAD_DIM), jnp.bfloat16),
            pltpu.SemaphoreType.DMA((5,)),
        ],
        compiler_params=params(32),
        cost_estimate=cost(0, 2**23),
        name="prefix_of_head",
    )(prefix_keys, prefix_values)


def dot_turned(keys, queries):
    return lax.dot_general(
        keys, queries, (((1,), (1,)), ((), ())), preferred_element_type=jnp.float32
    )


def score_tile(keys, queries, allowed, s_ref, peak_ref):
    scores = dot_turned(keys, queries)
    if allowed is not None:
        scores = jnp.where(allowed, scores, -jnp.inf)
    s_ref[...] = scores
    return jnp.max(scores.reshape(scores.shape[0] // 8, 8, scores.shape[1]), axis=0)


def weigh_tile(s_ref, peak_ref, values, b, old, m_ref, acc_ref, following):
    old_m, old_acc = old
    before = old_m[b, :1, :]
    peak = jnp.maximum(jnp.max(peak_ref[...], axis=0, keepdims=True), before)
    scaled = peak * EXP2_SCALE
    following_peak = following()
    parts = []
    for n in range(2):
        at = slice(n * (TILE // 2), (n + 1) * (TILE // 2))
        weights = jnp.exp2(s_ref[:, at] * EXP2_SCALE - scaled[:, at]).astype(jnp.bfloat16)
        parts.append(jnp.dot(values, weights, preferred_element_type=jnp.float32))
    sums = jnp.concatenate(parts, axis=1)
    if following_peak is not None:
        peak_ref[...] = following_peak
    acc_ref[b] = sums + old_acc[b] * jnp.exp2(before * EXP2_SCALE - scaled)
    m_ref[b] = jnp.broadcast_to(peak, m_ref.shape[1:])


def attend_prefix(span_start, got, prefix_keys, prefix_values):
    tokens, window = got.shape[0], prefix_keys.shape[0]
    blocks = tokens // TILE

    def kernel(start_ref, q_ref, k_ref, v_ref, m_ref, acc_ref, s_a, s_b, peak_ref):
        first_key = window - start_ref[0]
        m_ref[...] = jnp.full(m_ref.shape, LOWEST, jnp.float32)
        acc_ref[...] = jnp.zeros(acc_ref.shape, jnp.float32)
        opening = [
            jnp.minimum(jnp.maximum(b * TILE + 1, first_key) // TILE, window // TILE - 1)
            for b in range(blocks)
        ]
        ends = []
        for b in range(blocks):
            count = window // TILE - 1 - opening[b]
            ends.append(count if b == 0 else ends[-1] + count)

        def place(i):
            b = sum((i >= end).astype(jnp.int32) for end in ends)
            tile = jnp.int32(0)
            for n in range(blocks):
                start = 0 if n == 0 else ends[n - 1]
                tile = jnp.where(b == n, opening[n] + 1 + i - start, tile)
            return b, pl.multiple_of(tile * TILE, TILE)

        def score(b, row, s_ref, allowed=None):
            at = pl.ds(pl.multiple_of(jnp.minimum(b, blocks - 1) * TILE, TILE), TILE)
            return score_tile(
                k_ref[pl.ds(row, TILE), :], q_ref[at, :HEAD_DIM], allowed, s_ref, peak_ref
            )

        def score_opening(b, s_ref):
            row = pl.multiple_of(opening[b] * TILE, TILE)
            key = lax.broadcasted_iota(jnp.int32, (TILE, TILE), 0)
            query = lax.broadcasted_iota(jnp.int32, (1, TILE), 1) + b * TILE
            allowed = key >= jnp.maximum(query + 1, first_key) - row
            return score(b, row, s_ref, allowed)

        def weigh(b, row, s_ref, following):
            weigh_tile(
                s_ref,
                peak_ref,
                v_ref[:, pl.ds(row, TILE)],
                b,
                (m_ref, acc_ref),
                m_ref,
                acc_ref,
                following,
            )

        bufs = (s_a, s_b)
        peak_ref[...] = score_opening(0, s_a)
        for b in range(blocks):
            now, later = bufs[b % 2], bufs[(b + 1) % 2]
            if b + 1 < blocks:
                following = lambda b=b, later=later: score_opening(b + 1, later)
            else:
                following = lambda later=later: score(*place(jnp.int32(0)), later)
            weigh(b, pl.multiple_of(opening[b] * TILE, TILE), now, following)
        now, later = bufs[blocks % 2], bufs[(blocks + 1) % 2]

        def several(first, count):
            for n in range(0, count, 2):
                i = first + n
                weigh(*place(i), now, lambda i=i: score(*place(i + 1), later))
                weigh(*place(i + 1), later, lambda i=i: score(*place(i + 2), now))

        many = ends[-1] // UNROLL

        def unrolled(i, _):
            several(i * UNROLL, UNROLL)
            return 0

        def rest(i, _):
            several(many * UNROLL + 2 * i, 2)
            return 0

        lax.fori_loop(0, many, unrolled, 0)
        lax.fori_loop(0, (ends[-1] - many * UNROLL + 1) // 2, rest, 0)

    return pl.pallas_call(
        kernel,
        out_shape=[
            jax.ShapeDtypeStruct((blocks + 1, 8, TILE), jnp.float32),
            jax.ShapeDtypeStruct((blocks + 1, V_ROWS, TILE), jnp.float32),
        ],
        in_specs=[in_smem()] + [in_vmem()] * 3,
        out_specs=[in_vmem()] * 2,
        scratch_shapes=[
            pltpu.VMEM((TILE, TILE), jnp.float32),
            pltpu.VMEM((TILE, TILE), jnp.float32),
            pltpu.VMEM((8, TILE), jnp.float32),
        ],
        compiler_params=params(),
        cost_estimate=cost(4 * tokens * window * HEAD_DIM, 2**22),
        name="attend_prefix",
    )(span_start, got, prefix_keys, prefix_values)


def attend_span(got, other, m, acc):
    tokens = got.shape[0]
    blocks = tokens // TILE

    def kernel(got_ref, other_ref, m_in, acc_in, o_ref, m_ref, acc_ref, k_ref, v_ref, held, s_a, s_b, peak_ref):
        holds_values = lax.axis_index("seq") % 2
        v_ref[HEAD_DIM:, :] = jnp.ones((ONES_ROWS, tokens), jnp.bfloat16)

        @pl.when(holds_values == 0)
        def _():
            k_ref[...] = got_ref[:, HEAD_DIM:]
            held[...] = other_ref[...]

        @pl.when(holds_values == 1)
        def _():
            k_ref[...] = other_ref[...]
            held[...] = got_ref[:, HEAD_DIM:]

        tiles = [(b, b) for b in range(blocks)]
        tiles += [(b, j) for b in range(blocks) for j in range(b)]

        def score(n, s_ref):
            b, j = tiles[n]
            allowed = None
            if b == j:
                key = lax.broadcasted_iota(jnp.int32, (TILE, TILE), 0)
                query = lax.broadcasted_iota(jnp.int32, (TILE, TILE), 1)
                allowed = key <= query
            return score_tile(
                k_ref[j * TILE : (j + 1) * TILE, :],
                got_ref[b * TILE : (b + 1) * TILE, :HEAD_DIM],
                allowed,
                s_ref,
                peak_ref,
            )

        bufs = (s_a, s_b)
        peak_ref[...] = score(0, s_a)
        for n, (b, j) in enumerate(tiles):
            more = n + 1 < len(tiles)
            at = slice(j * TILE, (j + 1) * TILE)
            if b == j:
                v_ref[:HEAD_DIM, at] = held[at, :].T
            weigh_tile(
                bufs[n % 2],
                peak_ref,
                v_ref[:, j * TILE : (j + 1) * TILE],
                b,
                (m_in, acc_in) if b == j else (m_ref, acc_ref),
                m_ref,
                acc_ref,
                lambda n=n, more=more: score(n + 1, bufs[(n + 1) % 2]) if more else None,
            )
        for b in range(blocks):
            mixed = acc_ref[b, :HEAD_DIM, :] / acc_ref[b, HEAD_DIM : HEAD_DIM + 1, :]
            o_ref[b * TILE : (b + 1) * TILE, :] = mixed.T.astype(jnp.bfloat16)

    return pl.pallas_call(
        kernel,
        out_shape=jax.ShapeDtypeStruct((tokens, HEAD_DIM), jnp.bfloat16),
        in_specs=[in_vmem()] * 4,
        out_specs=in_vmem(),
        scratch_shapes=[
            pltpu.VMEM(m.shape, jnp.float32),
            pltpu.VMEM(acc.shape, jnp.float32),
            pltpu.VMEM((tokens, HEAD_DIM), jnp.bfloat16),
            pltpu.VMEM((V_ROWS, tokens), jnp.bfloat16),
            pltpu.VMEM((tokens, HEAD_DIM), jnp.bfloat16),
            pltpu.VMEM((TILE, TILE), jnp.float32),
            pltpu.VMEM((TILE, TILE), jnp.float32),
            pltpu.VMEM((8, TILE), jnp.float32),
        ],
        compiler_params=params(),
        cost_estimate=cost(2 * tokens * tokens * HEAD_DIM, 2**22),
        name="attend_span",
    )(got, other, m, acc)


def spread_shards(queries, keys, values, prefix_keys, prefix_values, span_start):
    rows = queries.shape[0]
    seq_size, head_size = lax.axis_size("seq"), lax.axis_size("head")
    tokens = seq_size * head_size * rows
    packed = pack_heads(queries, keys, values, seq_size, head_size)
    got = lax.all_to_all(packed, BOTH, split_axis=0, concat_axis=0, tiled=True)
    got = got.reshape(tokens, 2 * HEAD_DIM)
    head_keys, head_values = prefix_of_head(prefix_keys, prefix_values)
    got, head_keys, head_values = lax.optimization_barrier((got, head_keys, head_values))
    other = lax.ppermute(got[:, HEAD_DIM:], "seq", [(i, i ^ 1) for i in range(seq_size)])
    m, acc = attend_prefix(span_start, got, head_keys, head_values)
    attended = attend_span(got, other, m, acc)
    attended = attended.reshape(seq_size * head_size, rows, HEAD_DIM)
    back = lax.all_to_all(attended, BOTH, split_axis=0, concat_axis=0, tiled=True)
    return unpack_heads(back, seq_size, head_size)


def solution(mesh):
    placed = (
        P(("seq", "head"), None),
        P(("seq", "head"), None),
        P(("seq", "head"), None),
        P(None, "head"),
        P(None, "head"),
        P(),
    )
    fits = mesh.shape["seq"] * mesh.shape["head"] == QH and QH == 2 * KVH
    shards = spread_shards if fits else relayed_shards
    return jax.shard_map(
        shards, mesh=mesh, in_specs=placed, out_specs=P(("seq", "head"), None), check_vma=False
    )
```
